512 devices in a mesh: dp: 64 (over y_lo, z, core), mp: 8 (over x, y_hi).
Axes of the slice: x: 4, y: 4 (y_hi: 2, y_lo: 2; y = y_hi * 2 + y_lo), z: 16, core: 2. Of those that a mesh axis runs over, the one named last changes fastest.
Arguments:
- tokens: bfloat16 [16384, 4096], P('dp'), may hold values from -6 to 6
- hidden_grad: bfloat16 [16384, 8192], P('dp', 'mp'), may hold values from -6 to 6
- w_in: bfloat16 [4096, 8192], P('dp', 'mp'), may hold values from -0.09375 to 0.09375
- b_in: float32 [8192], P('mp'), may hold values from -4 to 4
- query_in: bfloat16 [2048, 4096], P('dp'), may hold values from -0.09375 to 0.09375
- query_hidden: bfloat16 [2048, 8192], P('dp', 'mp'), may hold values from -0.015625 to 0.015625
- owners: int32 [64], replicated, may hold values from 0 to 63, each once
- routes: int32 [16384, 1], P('dp'), may hold values from 0 to 63; in each aligned block of 256 rows (0 to 255, 256 to 511, ...) at most 8 rows name the same one
- example_slot: int32 [16384], P('dp'), may hold values from 0 to 7
Outputs:
- scores: float32 [512, 16], P('dp')
The draws below stay inside these ranges and needn't reach their ends.
Inputs may be any that keep to these rules, and one draw needn't show every extreme that they name: A permutation; batch b's factors are in slot owners[b]. `routes`: among the 256 tokens of one index of dp, no destination is named more than 8 times, a bound that some block reaches.
All inputs are finite; a program needn't handle non-finite values.
Results may differ from the reference program's by a relative error of at most 0.0003.
Values may be sent and summed in bfloat16 or wider, within the bound.
A program may use at most 64 MiB of HBM per device.

```python
import math
import jax
import jax.numpy as jnp
import numpy as np
from jax import lax

D = 4096
FF = 8192
ROWS_IN = 256
EX_OUT = 8
QB = 4
RANK = 8
NB = 4
CAP = 8
M = 32
TOKENS_IN = 16384
N_DP = 64


def with_ends(values, own_key, smallest, largest):
    index_at = [jax.random.randint(jax.random.fold_in(own_key, axis), (), 0, length) for axis, length in enumerate(values.shape)]
    widest = values.shape.index(max(values.shape))
    next_to = index_at[:widest] + [(index_at[widest] + 1) % values.shape[widest]] + index_at[widest + 1:]
    return values.at[tuple(index_at)].set(smallest).at[tuple(next_to)].set(largest)


def levels(own_key, extent, shards, low, largest):
    loudness = 1.0
    for axis_at, blocks in shards:
        draws = jax.random.uniform(jax.random.fold_in(jax.random.fold_in(own_key, 6), axis_at), (blocks,), jnp.float32, low / len(shards), largest / len(shards))
        loudness = loudness * jnp.repeat(jnp.exp(draws), extent[axis_at] // blocks).reshape((-1,) + (1,) * (len(extent) - 1 - axis_at))
    return loudness


def deal_out(stream_key, own, number, rows, amount, top, limit, skew):
    sequence = jax.random.permutation(stream_key, amount)
    packed, common = load_shares(amount, rows * top, limit, skew, True), load_shares(amount, rows * top, limit, skew, False)
    places = jnp.arange(amount)

    def named(sizes, rotation):
        used = int((sizes > 0).sum())
        fixed = max(1, used // 4)
        moved = fixed + (places - fixed + rotation * (used - fixed)) % max(1, amount - fixed)
        return jnp.zeros((amount,), jnp.int32).at[sequence[jnp.where(places < fixed, places, moved)]].set(jnp.asarray(sizes, jnp.int32))

    sizes = jnp.where(number % 4 == 0, named(packed, number // 4), named(common, number - number // 4 - 1))
    mixed = jax.random.permutation(jax.random.fold_in(own, 3), amount)
    giver, taker = mixed[0:amount // 2 * 2:2], mixed[1:amount // 2 * 2:2]
    margin = jnp.minimum(sizes[giver] - 1, limit - sizes[taker]) // 2
    margin = jnp.where((giver == sequence[0]) | (taker == sequence[0]) | (sizes[taker] == 0), 0, jnp.maximum(margin, 0))
    moved = jax.random.randint(jax.random.fold_in(own, 4), (amount // 2,), 0, 1 << 20) % (margin + 1)
    sizes = sizes.at[giver].add(-moved).at[taker].add(moved)
    items = jnp.searchsorted(jnp.cumsum(sizes), jnp.arange(rows * top), side="right").astype(jnp.int32)
    table = items.reshape(top, rows).T
    table = table[jax.random.permutation(jax.random.fold_in(own, 1), rows)]
    rotation = jax.random.randint(jax.random.fold_in(own, 2), (rows, 1), 0, top)
    return jnp.take_along_axis(table, (jnp.arange(top)[None, :] + rotation) % top, axis=1)


def load_shares(amount, total, most, skew, full):
    loads = [(1 << 20) // math.isqrt(rank ** skew) + 1 for rank in range(1, amount + 1)]
    largest = most if full else min(most, max(-(-total // amount), total * loads[0] // sum(loads)))
    least = 1 if total - largest >= amount - 1 else 0
    holding, surplus = [largest] + [least] * (amount - 1), total - largest - least * (amount - 1)
    while surplus > 0:
        movable = [i for i in range(1, amount) if holding[i] < largest] or [i for i in range(1, amount) if holding[i] < most]
        mass, budget = sum([loads[i] for i in movable]), surplus
        for i in movable:
            extra = min(most - holding[i], max(1, budget * loads[i] // mass), surplus)
            holding[i] = holding[i] + extra
            surplus = surplus - extra
    return np.array(holding)


def gaussian(key, dims, spread, limit, shards=(), held_as=jnp.bfloat16):
    drawn = jax.random.normal(key, dims, jnp.float32) * spread
    if len(shards) > 0:
        drawn = levels(key, dims, shards, -0.22, 0.18) * drawn
    return jnp.clip(drawn, min=-limit, max=limit).astype(held_as)


def setup_inputs(seed: int = 0) -> dict:
    key_list = jax.random.split(jax.random.key(seed), 10)
    tokens = gaussian(key_list[0], (TOKENS_IN, D), 1.0, 6.0, ((0, 64),))
    hidden_grad = gaussian(key_list[1], (TOKENS_IN, FF), 1.0, 6.0, ((0, 64), (1, 8)))
    w_in = gaussian(key_list[2], (D, FF), D ** -0.5, 0.09375, ((0, 64), (1, 8)))
    b_in = gaussian(key_list[3], (FF,), 1.0, 4.0, ((0, 8),), jnp.float32)
    query_in = gaussian(key_list[4], (N_DP * M, D), D ** -0.5, 0.09375, ((0, 64),))
    query_hidden = gaussian(key_list[5], (N_DP * M, FF), (16 * FF) ** -0.5, 0.015625, ((0, 64), (1, 8)))
    owners = jax.random.permutation(key_list[6], N_DP).astype(jnp.int32)
    routes_keys = jax.random.split(jax.random.fold_in(key_list[7], 1), TOKENS_IN // ROWS_IN)
    routes_turns = jax.random.permutation(jax.random.fold_in(key_list[7], 3), TOKENS_IN // ROWS_IN)
    routes = jax.vmap(lambda own, number: deal_out(jax.random.fold_in(key_list[7], 2), own, number, ROWS_IN, N_DP, 1, CAP, 1))(routes_keys, routes_turns).reshape((TOKENS_IN, 1))
    example_slot = with_ends(jax.random.randint(key_list[8], (TOKENS_IN,), 0, EX_OUT), jax.random.fold_in(key_list[8], 1), 0, EX_OUT - 1).astype(jnp.int32)
    return {"tokens": tokens, "hidden_grad": hidden_grad, "w_in": w_in, "b_in": b_in, "query_in": query_in, "query_hidden": query_hidden, "owners": owners, "routes": routes, "example_slot": example_slot}


def slope(pre):
    cdf = 0.5 * (1.0 + jax.scipy.special.erf(pre * 0.7071067811865476))
    dens = jnp.exp(-0.5 * pre * pre) * 0.3989422804014327
    return cdf + pre * dens


def reference(tokens, hidden_grad, w_in, b_in, query_in, query_hidden, owners, routes, example_slot):
    rows_batch = QB * RANK
    lefts = []
    rights = []
    for batch in range(NB):
        start = (owners[batch] * rows_batch).astype(jnp.int32)
        lefts.append(lax.dynamic_slice_in_dim(query_in, start, rows_batch, 0))
        rights.append(lax.dynamic_slice_in_dim(query_hidden, start, rows_batch, 0))
    factors_in = jnp.concatenate(lefts, axis=0)
    factors_hidden = jnp.concatenate(rights, axis=0).astype(jnp.float32)

    def block(pair):
        rows, grads = pair
        pre = jnp.dot(rows, w_in, preferred_element_type=jnp.float32) + b_in
        delta = grads.astype(jnp.float32) * slope(pre)
        left = jnp.dot(rows, factors_in.T, preferred_element_type=jnp.float32)
        right = jnp.dot(delta, factors_hidden.T, precision=lax.Precision.HIGHEST)
        return (left * right).reshape(rows.shape[0], NB * QB, RANK).sum(axis=-1)

    contrib = lax.map(block, (tokens.reshape(N_DP, ROWS_IN, D), hidden_grad.reshape(N_DP, ROWS_IN, FF)))
    contrib = contrib.reshape(N_DP * ROWS_IN, NB * QB)
    keys = (routes[:, 0] * EX_OUT + example_slot).astype(jnp.int32)
    return jax.ops.segment_sum(contrib, keys, num_segments=N_DP * EX_OUT)
```

```python
import functools

import jax
import jax.numpy as jnp
from jax import lax
from jax.experimental import pallas as pl
from jax.experimental.pallas import tpu as pltpu
from jax.sharding import PartitionSpec as P

MESH = pl.DeviceIdType.MESH
RANK = 8
EX_OUT = 8
NT = (((1,), (1,)), ((), ()))


def slope(pre):
    cdf = 0.5 * (1.0 + lax.erf(pre * 0.7071067811865476))
    dens = jnp.exp(-0.5 * pre * pre) * 0.3989422804014327
    return cdf + pre * dens


def kernel(
    X, YH, Z, NB,
    owners, tokens, hg, w, bias, qi, qh, meta, out,
    wbuf, tok2, acc, hg2, dhi, dlo, meta2,
    qi_raw, qh_raw, gbuf, rs_in, red, fbuf, fsib, fpair, left_all,
    terms, t1_in, psum, t2_in,
    ring_s, ring_r, sib_s, sib_r, tok_s, tok_r, pair_s, pair_r, quad_s, quad_r,
    rs_s, rs_r, ag_s, ag_r, fq_s, fq_r, lf_s, lf_r, t1_s, t1_r, t2_s, t2_r, loc_s,
):
    NY, S, NC = 2 * YH, Z // 2, 2 * NB
    T, D = tokens.shape
    WR, H = w.shape[0], w.shape[1] // 2
    QC = H // 2
    NPL = X * NY * 2
    R = Z // NC
    dp, mp = lax.axis_index("dp"), lax.axis_index("mp")
    c = lax.rem(dp, 2)
    z = lax.rem(lax.div(dp, 2), Z)
    yl = lax.div(dp, 2 * Z)
    yh = lax.rem(mp, YH)
    x = lax.div(mp, YH)
    y = yh * 2 + yl
    me_pl = (x * NY + y) * 2 + c
    quarter = yl * 2 + c

    def dev(x_, y_, z_, c_):
        return ((lax.rem(y_, 2) * Z + z_) * 2 + c_, x_ * YH + lax.div(y_, 2))

    def zpeer(k):
        return dev(x, y, lax.rem(z + k, Z), c)

    def plane(k):
        i = lax.rem(me_pl + k, NPL)
        return dev(lax.div(i, NY * 2), lax.rem(lax.div(i, 2), NY), z, lax.rem(i, 2))

    def remote(src, dst, send, recv, to):
        return pltpu.make_async_remote_copy(
            src_ref=src, dst_ref=dst, send_sem=send, recv_sem=recv,
            device_id=to, device_id_type=MESH,
        )

    def loop(n, f, start=0):
        def step(i, carry):
            f(i)
            return carry

        lax.fori_loop(start, n, step, 0)

    barrier = pltpu.get_barrier_semaphore()
    loop(Z, lambda k: pl.semaphore_signal(barrier, inc=1, device_id=zpeer(k), device_id_type=MESH), 1)
    loop(NPL, lambda k: pl.semaphore_signal(barrier, inc=1, device_id=plane(k), device_id_type=MESH), 1)
    pl.semaphore_wait(barrier, Z - 1 + NPL - 1)

    sibling = dev(x, y, z, 1 - c)
    partner = dev(x, yh * 2 + 1 - yl, z, c)
    up, down = zpeer(1), zpeer(Z - 1)
    y_up = dev(x, lax.rem(y + 1, NY), z, c)
    y_down = dev(x, lax.rem(y + NY - 1, NY), z, c)

    def half(i):
        return pl.ds(pl.multiple_of(i * H, H), H)

    pair_w = remote(w.at[:, half(1 - yl)], wbuf.at[z, yl, c], pair_s.at[0], pair_r.at[0], partner)
    pair_w.start()
    wbuf[z, yl, c] = w[:, half(yl)]

    def at(direction, s):
        return lax.rem(z + (Z - s if direction == 0 else s), Z)

    def ring(direction, a, s):
        ref = wbuf.at[at(direction, s - 1), a, c]
        return remote(
            ref, ref, ring_s.at[direction, a, s], ring_r.at[direction, a, s], (up, down)[direction]
        )

    def sib(direction, a, s):
        ref = wbuf.at[at(direction, s), a, c]
        return remote(ref, ref, sib_s.at[direction, a, s], sib_r.at[direction, a, s], sibling)

    def hops(direction, a):
        return S if direction == a else S - 1

    def cols(direction, s, h):
        return pl.ds(pl.multiple_of(h * (D // 2) + at(direction, s) * 2 * WR, 2 * WR), 2 * WR)

    def tok(direction, s, h):
        k = cols(direction, s, h)
        return remote(
            tokens.at[:, k], tok2.at[:, k], tok_s.at[direction, s, h], tok_r.at[direction, s, h],
            (y_up, y_down)[direction],
        )

    def tok_start(direction, s):
        if (1 if direction == 0 else 0) <= s <= (S if direction == 0 else S - 1):
            tok(direction, s, 0).start()
            tok(direction, s, 1).start()

    def first(a):
        ring(0, a, 1).start()
        ring(1, a, 1).start()
        sib(0, a, 0).start()

    first(yl)

    b_mine, h_mine = lax.div(mp, 2), lax.rem(mp, 2)
    qrows = pl.ds(pl.multiple_of(h_mine * 16, 16), 16)

    def quad_of(k):
        q = lax.rem(quarter + k, 4)
        return q, dev(x, yh * 2 + lax.div(q, 2), z, lax.rem(q, 2))

    def quad(k):
        q, to = quad_of(k)
        a = remote(
            qi.at[qrows, pl.ds(pl.multiple_of(q * (D // 4), 128), D // 4)], qi_raw.at[k],
            quad_s.at[0, k], quad_r.at[0, k], to,
        )
        b = remote(
            qh.at[:, pl.ds(pl.multiple_of(q * QC, 128), QC)], qh_raw.at[k],
            quad_s.at[1, k], quad_r.at[1, k], to,
        )
        return a, b

    for k in (1, 2, 3):
        for cp in quad(k):
            cp.start()
    qi_raw[0] = qi[qrows, pl.ds(pl.multiple_of(quarter * (D // 4), 128), D // 4)]
    qh_raw[0] = qh[:, pl.ds(pl.multiple_of(quarter * QC, 128), QC)]
    pair_meta = remote(meta, meta2, pair_s.at[1], pair_r.at[1], partner)
    pair_meta.start()

    pair_w.wait_recv()
    first(1 - yl)
    for s in (0, 1, 2):
        tok_start(0, s)
        tok_start(1, s)
    pair_hg = remote(hg.at[:, half(1 - yl)], hg2, pair_s.at[2], pair_r.at[2], partner)

    for k in (1, 2, 3):
        for cp in quad(k):
            cp.wait_recv()
    srcs = []
    for k in range(4):
        q = lax.rem(quarter + 4 - k, 4)
        srcs.append((lax.div(q, 2) * Z + z) * 2 + lax.rem(q, 2))

    def pick(b, k):
        return jnp.where(owners[b] == srcs[k], 1.0, 0.0).astype(jnp.float32)

    for i in range(NC):
        b, h = i // 2, i % 2
        gi = sum(pick(b_mine, k) * qi_raw[k, :, i * 128 : (i + 1) * 128].astype(jnp.float32) for k in range(4))
        gh = sum(pick(b, k) * qh_raw[k, h * 16 : (h + 1) * 16].astype(jnp.float32) for k in range(4))
        gbuf[i, :, :128] = gi.astype(jnp.bfloat16)
        gbuf[i, :, 128:] = gh.astype(jnp.bfloat16)

    is_red = lax.rem(z, R) == 0
    my_chunk = lax.div(z, R)

    def rs(i):
        k = lax.rem(z + Z - i * R, Z)
        return remote(gbuf.at[i], rs_in.at[k], rs_s.at[i], rs_r.at[k], dev(x, y, i * R, c))

    def rs_arrived(k):
        return remote(gbuf.at[0], rs_in.at[k], rs_s.at[0], rs_r.at[k], up)

    def ag(k):
        return remote(red, fbuf.at[my_chunk], ag_s.at[k], ag_r.at[my_chunk], zpeer(k))

    def ag_arrived(i):
        return remote(red, fbuf.at[i], ag_s.at[0], ag_r.at[i], up)

    def not_mine(f):
        def go(i):
            @pl.when(i * R != z)
            def _():
                f(i)

        return go

    loop(NC, not_mine(lambda i: rs(i).start()))

    def reduce_factors():
        @pl.when(is_red)
        def _():
            def add(k, total):
                rs_arrived(k).wait_recv()
                return total + rs_in[k].astype(jnp.float32)

            total = lax.fori_loop(1, Z, add, gbuf[my_chunk].astype(jnp.float32))
            red[...] = total.astype(jnp.bfloat16)
            fbuf[my_chunk] = total.astype(jnp.bfloat16)
            loop(Z, lambda k: ag(k).start(), 1)

    def fq(k):
        _, to = quad_of(k)
        return remote(fbuf.at[:, :, pl.ds(0, 128)], fpair.at[k - 1], fq_s.at[k], fq_r.at[k], to)

    fh_sib = remote(fbuf.at[:, :, pl.ds(128, QC)], fsib, fq_s.at[0], fq_r.at[0], sibling)

    def gather_factors():
        loop(NC, not_mine(lambda i: ag_arrived(i).wait_recv()))
        fh_sib.start()
        for k in (1, 2, 3):
            fq(k).start()

    def lf(k):
        n_y = NPL // 2
        i = lax.rem(lax.div(me_pl, 2) + k, n_y)
        to = dev(lax.div(i, NY), lax.rem(i, NY), z, c)
        ref = left_all.at[yl, mp]
        return remote(ref, ref, lf_s.at[k], lf_r.at[k], to)

    def lf_arrived(k):
        n_y = NPL // 2
        i = lax.rem(lax.div(me_pl, 2) + n_y - k, n_y)
        ref = left_all.at[lax.rem(i, 2), lax.div(i, NY) * YH + lax.div(lax.rem(i, NY), 2)]
        return remote(ref, ref, lf_s.at[k], lf_r.at[k], up)

    def left_part():
        total = jnp.zeros((16, T), jnp.float32)
        for k in range(4):
            q = lax.rem(quarter + 4 - k, 4)
            if k:
                fq(k).wait_recv()
            for i in range(NC):
                f = fbuf[i, :, :128] if k == 0 else fpair[k - 1, i]
                kk = pl.ds(pl.multiple_of(q * (D // 4) + i * 128, 128), 128)
                total = total + lax.dot_general(f, tokens[:, kk], NT, preferred_element_type=jnp.float32)
        left_all[yl, mp] = total
        loop(NPL // 2, lambda k: lf(k).start(), 1)

    def multiply(direction, s):
        for a in (0, 1):
            if s == 0:
                sib(0, a, 0).wait_recv()
            elif s <= hops(direction, a):
                sib(direction, a, s).wait_recv()
            elif s == S:
                sib(1 - direction, a, s).wait_recv()
        block = wbuf[at(direction, s)].reshape(4 * WR, H)
        k0, k1 = cols(direction, s, 0), cols(direction, s, 1)
        own = jnp.concatenate([tokens[:, k0], tokens[:, k1]], axis=1)
        acc[0] = acc[0] + jnp.dot(own, block, preferred_element_type=jnp.float32)
        tok(direction, s, 0).wait_recv()
        tok(direction, s, 1).wait_recv()
        other = jnp.concatenate([tok2[:, k0], tok2[:, k1]], axis=1)
        acc[1] = acc[1] + jnp.dot(other, block, preferred_element_type=jnp.float32)

    def advance(direction, a, s):
        if s <= hops(direction, a):
            ring(direction, a, s).wait_recv()
            if s + 1 <= hops(direction, a):
                ring(direction, a, s + 1).start()
            sib(direction, a, s).start()

    acc[...] = jnp.zeros_like(acc)
    for s in range(1, S + 1):
        for direction, a in ((0, 0), (1, 1), (0, 1), (1, 0)):
            advance(direction, a, s)
        if s + 2 <= S:
            tok_start(0, s + 2)
            tok_start(1, s + 2)
        if s == min(2, S):
            pair_hg.start()
        if s == min(3, S):
            reduce_factors()
        if s == min(5, S):
            gather_factors()
        if s == min(6, S):
            left_part()
        if s == 1:
            multiply(1, 0)
        else:
            multiply(0, s - 1)
            multiply(1, s - 1)
    multiply(0, S)

    pair_hg.wait_recv()
    pair_meta.wait_recv()
    fh_sib.wait_recv()
    fh_own = fbuf[:, :, 128:].reshape(NC * 16, QC)
    fh_other = fsib[...].reshape(NC * 16, QC)
    fh = jnp.concatenate([jnp.where(c == 0, fh_own, fh_other), jnp.where(c == 0, fh_other, fh_own)], axis=1)
    shift = bias[:, half(yl)]
    rows = 32
    for g in (0, 1):

        def some(i, carry, g=g):
            at_rows = pl.ds(pl.multiple_of(i * rows, rows), rows)
            grads = hg[at_rows, half(yl)] if g == 0 else hg2[at_rows, :]
            delta = grads.astype(jnp.float32) * slope(acc[g, at_rows, :] + shift)
            high = delta.astype(jnp.bfloat16)
            dhi[g, at_rows, :] = high
            dlo[g, at_rows, :] = (delta - high.astype(jnp.float32)).astype(jnp.bfloat16)
            return carry

        lax.fori_loop(0, T // rows, some, 0)
    loop(NPL // 2, lambda k: lf_arrived(k).wait_recv(), 1)
    total = jnp.zeros((Z * 4, 128), jnp.float32)
    n_q = NC * 16 // RANK
    for g in (0, 1):
        right = lax.dot_general(fh, dhi[g], NT, preferred_element_type=jnp.float32)
        right = right + lax.dot_general(fh, dlo[g], NT, preferred_element_type=jnp.float32)
        left = left_all[yl if g == 0 else 1 - yl].reshape(NC * 16, T)
        contrib = (left * right).reshape(n_q, RANK, T).sum(axis=1)
        keys = meta[...] if g == 0 else meta2[...]
        wide = jnp.concatenate([contrib] * (128 // n_q), axis=0)
        slot_of = lax.div(lax.broadcasted_iota(jnp.int32, (128, T), 0), n_q)
        wide = jnp.where(slot_of == keys[1:2], wide, 0.0)
        place = lax.broadcasted_iota(jnp.int32, (Z * 4, T), 0)
        named = jnp.where(place == keys[0:1], 1.0, 0.0).astype(jnp.bfloat16)
        high = wide.astype(jnp.bfloat16)
        rest = wide - high.astype(jnp.float32)
        mid = rest.astype(jnp.bfloat16)
        low = (rest - mid.astype(jnp.float32)).astype(jnp.bfloat16)
        for part in (high, mid, low):
            total = total + lax.dot_general(named, part, NT, preferred_element_type=jnp.float32)
    for i in range(Z):
        terms[i] = total[i * 4 : i * 4 + 4]

    def t1(k):
        return remote(terms.at[lax.rem(z + k, Z)], t1_in.at[k], t1_s.at[k], t1_r.at[k], zpeer(k))

    def t2(k):
        return remote(psum, t2_in.at[k], t2_s.at[k], t2_r.at[k], plane(k))

    loop(Z, lambda k: t1(k).start(), 1)

    def add1(k, total):
        t1(k).wait_recv()
        return total + t1_in[k]

    mine = lax.fori_loop(1, Z, add1, terms[z])
    psum[...] = mine
    loop(NPL, lambda k: t2(k).start(), 1)

    def add2(k, total):
        t2(k).wait_recv()
        return total + t2_in[k]

    mine = lax.fori_loop(1, NPL, add2, mine)
    row = lax.broadcasted_iota(jnp.int32, (4, 128), 0)
    out[...] = jnp.sum(jnp.where(row == quarter, mine, 0.0), axis=0, keepdims=True)

    for cp in (pair_w, pair_meta, pair_hg, fh_sib):
        cp.wait_send()
    for direction in (0, 1):
        for a in (0, 1):
            for s in range(1, hops(direction, a) + 1):
                ring(direction, a, s).wait_send()
                sib(direction, a, s).wait_send()
    for a in (0, 1):
        sib(0, a, 0).wait_send()
    for direction in (0, 1):
        for s in range(1 - direction, S + 1 - direction):
            for h in (0, 1):
                tok(direction, s, h).wait_send()
    for k in (1, 2, 3):
        for cp in quad(k):
            cp.wait_send()
        fq(k).wait_send()
    loop(NC, not_mine(lambda i: rs(i).wait_send()))

    @pl.when(is_red)
    def _():
        loop(Z, lambda k: ag(k).wait_send(), 1)

    loop(NPL // 2, lambda k: lf(k).wait_send(), 1)
    loop(Z, lambda k: t1(k).wait_send(), 1)
    loop(NPL, lambda k: t2(k).wait_send(), 1)


def body(X, YH, Z, tokens, hidden_grad, w_in, b_in, query_in, query_hidden, owners, routes, example_slot):
    T, D = tokens.shape
    M = query_in.shape[0]
    NB = X * YH * 16 // M
    H = w_in.shape[1] // 2
    QC = H // 2
    NC = 2 * NB
    NY, S = 2 * YH, Z // 2
    NPL = X * NY * 2
    dest = routes[:, 0]
    place = lax.rem(lax.div(dest, 2), Z) * 4 + lax.div(dest, 2 * Z) * 2 + lax.rem(dest, 2)
    meta = jnp.concatenate([place[None], example_slot[None], jnp.zeros((6, T), jnp.int32)])
    bf, f32 = jnp.bfloat16, jnp.float32
    dma = pltpu.SemaphoreType.DMA
    vmem = pl.BlockSpec(memory_space=pltpu.VMEM)
    scratch = [
        pltpu.VMEM((Z, 2, 2, w_in.shape[0], H), bf),
        pltpu.VMEM((T, D), bf),
        pltpu.VMEM((2, T, H), f32),
        pltpu.VMEM((T, H), bf),
        pltpu.VMEM((2, T, H), bf),
        pltpu.VMEM((2, T, H), bf),
        pltpu.VMEM((8, T), jnp.int32),
        pltpu.VMEM((4, 16, D // 4), bf),
        pltpu.VMEM((4, M, QC), bf),
        pltpu.VMEM((NC, 16, 128 + QC), bf),
        pltpu.VMEM((Z, 16, 128 + QC), bf),
        pltpu.VMEM((16, 128 + QC), bf),
        pltpu.VMEM((NC, 16, 128 + QC), bf),
        pltpu.VMEM((NC, 16, QC), bf),
        pltpu.VMEM((3, NC, 16, 128), bf),
        pltpu.VMEM((2, X * YH, 16, T), f32),
        pltpu.VMEM((Z, 4, 128), f32),
        pltpu.VMEM((Z, 4, 128), f32),
        pltpu.VMEM((4, 128), f32),
        pltpu.VMEM((NPL, 4, 128), f32),
    ]
    scratch += [dma((2, 2, S + 1))] * 4 + [dma((2, S + 1, 2))] * 2 + [dma((3,))] * 2
    scratch += [dma((2, 4))] * 2 + [dma((NC,)), dma((Z,)), dma((Z,)), dma((NC,))] + [dma((4,))] * 2
    scratch += [dma((NPL // 2,))] * 2 + [dma((Z,))] * 2 + [dma((NPL,))] * 2 + [dma((1,))]
    scores = pl.pallas_call(
        functools.partial(kernel, X, YH, Z, NB),
        out_shape=jax.ShapeDtypeStruct((1, 128), f32),
        in_specs=[pl.BlockSpec(memory_space=pltpu.SMEM)] + [vmem] * 7,
        out_specs=vmem,
        scratch_shapes=scratch,
        compiler_params=pltpu.CompilerParams(
            collective_id=0, has_side_effects=True, vmem_limit_bytes=48 * 2**20
        ),
    )(owners, tokens, hidden_grad, w_in, b_in[None], query_in, query_hidden, meta)
    n_q = NC * 16 // RANK
    return scores[:, : EX_OUT * n_q].reshape(EX_OUT, n_q)


def solution(mesh, YH=2):
    Z = mesh.shape["dp"] // 4
    X = mesh.shape["mp"] // YH
    in_specs = (
        P("dp", None), P("dp", "mp"), P("dp", "mp"), P("mp"), P("dp", None), P("dp", "mp"), P(),
        P("dp", None), P("dp"),
    )
    return jax.shard_map(
        functools.partial(body, X, YH, Z), mesh=mesh, in_specs=in_specs, out_specs=P("dp", None), check_vma=False
    )
```

```python
import functools

import jax
import jax.numpy as jnp
from jax import lax
from jax.experimental import pallas as pl
from jax.experimental.pallas import tpu as pltpu
from jax.sharding import PartitionSpec as P

MESH = pl.DeviceIdType.MESH
RANK = 8
EX_OUT = 8
NT = (((1,), (1,)), ((), ()))


def slope(pre):
    cdf = 0.5 * (1.0 + lax.erf(pre * 0.7071067811865476))
    dens = jnp.exp(-0.5 * pre * pre) * 0.3989422804014327
    return cdf + pre * dens


def kernel(
    X, YH, Z, NB,
    owners_in, tok_in, hg_in, w, bias_in, qi, qh, routes, slots, out,
    owners, tokens, hg, bias, keys,
    wbuf, tok2, acc, hg2, dhi, dlo,
    qi_raw, qh_raw, gbuf, rs_in, red, fbuf, fsib, fpair, left_all,
    terms, t1_in, psum, t2_in,
    ring_s, ring_r, sib_s, sib_r, tok_s, tok_r, pair_s, pair_r, quad_s, quad_r,
    rs_s, rs_r, ag_s, ag_r, fq_s, fq_r, lf_s, lf_r, t1_s, t1_r, t2_s, t2_r, loc_s, know,
):
    NY, S, NC = 2 * YH, Z // 2, 2 * NB
    T, D = tok_in.shape
    WR, H = w.shape[0], w.shape[1] // 2
    QC = H // 2
    NPL = X * NY * 2
    R = Z // NC
    dp, mp = lax.axis_index("dp"), lax.axis_index("mp")
    c = lax.rem(dp, 2)
    z = lax.rem(lax.div(dp, 2), Z)
    yl = lax.div(dp, 2 * Z)
    yh = lax.rem(mp, YH)
    x = lax.div(mp, YH)
    y = yh * 2 + yl
    me_pl = (x * NY + y) * 2 + c
    quarter = yl * 2 + c

    def dev(x_, y_, z_, c_):
        return ((lax.rem(y_, 2) * Z + z_) * 2 + c_, x_ * YH + lax.div(y_, 2))

    def zpeer(k):
        return dev(x, y, lax.rem(z + k, Z), c)

    def plane(k):
        i = lax.rem(me_pl + k, NPL)
        return dev(lax.div(i, NY * 2), lax.rem(lax.div(i, 2), NY), z, lax.rem(i, 2))

    def remote(src, dst, send, recv, to):
        return pltpu.make_async_remote_copy(
            src_ref=src, dst_ref=dst, send_sem=send, recv_sem=recv,
            device_id=to, device_id_type=MESH,
        )

    def loop(n, f, start=0):
        def step(i, carry):
            f(i)
            return carry

        lax.fori_loop(start, n, step, 0)

    b_mine, h_mine = lax.div(mp, 2), lax.rem(mp, 2)
    qrows = pl.ds(pl.multiple_of(h_mine * 16, 16), 16)

    def half(i):
        return pl.ds(pl.multiple_of(i * H, H), H)

    locals_ = [
        (w.at[:, half(yl)], wbuf.at[z, yl, c]),
        (qi.at[qrows, pl.ds(pl.multiple_of(quarter * (D // 4), 128), D // 4)], qi_raw.at[0]),
        (qh.at[:, pl.ds(pl.multiple_of(quarter * QC, 128), QC)], qh_raw.at[0]),
        (owners_in, owners),
        (tok_in, tokens),
        (hg_in.at[:, half(yl)], hg),
        (bias_in.at[:, half(yl)], bias),
        (routes, keys.at[0]),
        (slots, keys.at[1]),
    ]
    own = [pltpu.make_async_copy(src, dst, loc_s.at[i]) for i, (src, dst) in enumerate(locals_)]
    for cp in own:
        cp.start()

    def steps(n, k):
        return sorted({k % n, -k % n} - {0}) if k < n else []

    def circle(kx, ky, kz, core):
        found = [dev(lax.rem(x + k, X), y, z, c) for k in (steps(X, kx) if kx else [])]
        found += [dev(x, lax.rem(y + k, NY), z, c) for k in (steps(NY, ky) if ky else [])]
        found += [zpeer(k) for k in (steps(Z, kz) if kz else [])]
        return found + ([dev(x, y, z, 1 - c)] if core else [])

    def tell(sem, devices):
        for to in devices:
            pl.semaphore_signal(sem, inc=1, device_id=to, device_id_type=MESH)

    near = circle(1, 1, 1, True)
    far2 = circle(2, 2, 2, True)
    far4 = circle(0, 0, 4, True)
    barrier = pltpu.get_barrier_semaphore()
    tell(barrier, near)
    pl.semaphore_wait(barrier, len(near))

    sibling = dev(x, y, z, 1 - c)
    partner = dev(x, yh * 2 + 1 - yl, z, c)
    up, down = zpeer(1), zpeer(Z - 1)
    y_up = dev(x, lax.rem(y + 1, NY), z, c)
    y_down = dev(x, lax.rem(y + NY - 1, NY), z, c)

    pair_w = remote(w.at[:, half(1 - yl)], wbuf.at[z, yl, c], pair_s.at[0], pair_r.at[0], partner)
    pair_w.start()
    own[0].wait()

    def at(direction, s):
        return lax.rem(z + (Z - s if direction == 0 else s), Z)

    def ring(direction, a, s):
        ref = wbuf.at[at(direction, s - 1), a, c]
        return remote(
            ref, ref, ring_s.at[direction, a, s], ring_r.at[direction, a, s], (up, down)[direction]
        )

    def sib(direction, a, s):
        ref = wbuf.at[at(direction, s), a, c]
        return remote(ref, ref, sib_s.at[direction, a, s], sib_r.at[direction, a, s], sibling)

    def hops(direction, a):
        return S if direction == a else S - 1

    def cols(direction, s, h):
        return pl.ds(pl.multiple_of(h * (D // 2) + at(direction, s) * 2 * WR, 2 * WR), 2 * WR)

    def tok(direction, s, h):
        k = cols(direction, s, h)
        return remote(
            tokens.at[:, k], tok2.at[:, k], tok_s.at[direction, s, h], tok_r.at[direction, s, h],
            (y_up, y_down)[direction],
        )

    def tok_start(direction, s):
        if (1 if direction == 0 else 0) <= s <= (S if direction == 0 else S - 1):
            tok(direction, s, 0).start()
            tok(direction, s, 1).start()

    def first(a):
        ring(0, a, 1).start()
        ring(1, a, 1).start()
        sib(0, a, 0).start()

    first(yl)
    tell(know.at[0], near)

    def quad_of(k):
        q = lax.rem(quarter + k, 4)
        return q, dev(x, yh * 2 + lax.div(q, 2), z, lax.rem(q, 2))

    def quad(k):
        q, to = quad_of(k)
        a = remote(
            qi.at[qrows, pl.ds(pl.multiple_of(q * (D // 4), 128), D // 4)], qi_raw.at[k],
            quad_s.at[0, k], quad_r.at[0, k], to,
        )
        b = remote(
            qh.at[:, pl.ds(pl.multiple_of(q * QC, 128), QC)], qh_raw.at[k],
            quad_s.at[1, k], quad_r.at[1, k], to,
        )
        return a, b

    pair_routes = remote(routes, keys.at[2], pair_s.at[1], pair_r.at[1], partner)
    pair_routes.start()
    pair_slots = remote(slots, keys.at[3], pair_s.at[3], pair_r.at[3], partner)
    pair_slots.start()

    pair_w.wait_recv()
    first(1 - yl)
    own[4].wait()
    for s in (0, 1, 2):
        tok_start(0, s)
        tok_start(1, s)
    pair_hg = remote(hg_in.at[:, half(1 - yl)], hg2, pair_s.at[2], pair_r.at[2], partner)

    pl.semaphore_wait(know.at[0], len(near))
    for k in (1, 2, 3):
        for cp in quad(k):
            cp.start()
    tell(know.at[1], far2)

    def pick_factors():
        for k in (1, 2, 3):
            for cp in quad(k):
                cp.wait_recv()
        for i in (1, 2, 3):
            own[i].wait()
        srcs = []
        for k in range(4):
            q = lax.rem(quarter + 4 - k, 4)
            srcs.append((lax.div(q, 2) * Z + z) * 2 + lax.rem(q, 2))

        def pick(b, k):
            return jnp.where(owners[b] == srcs[k], 1.0, 0.0).astype(jnp.float32)

        for i in range(NC):
            b, h = i // 2, i % 2
            gi = sum(pick(b_mine, k) * qi_raw[k, :, i * 128 : (i + 1) * 128].astype(jnp.float32) for k in range(4))
            gh = sum(pick(b, k) * qh_raw[k, h * 16 : (h + 1) * 16].astype(jnp.float32) for k in range(4))
            gbuf[i, :, :128] = gi.astype(jnp.bfloat16)
            gbuf[i, :, 128:] = gh.astype(jnp.bfloat16)

    is_red = lax.rem(z, R) == 0
    my_chunk = lax.div(z, R)

    def rs(i):
        k = lax.rem(z + Z - i * R, Z)
        return remote(gbuf.at[i], rs_in.at[k], rs_s.at[i], rs_r.at[k], dev(x, y, i * R, c))

    def rs_arrived(k):
        return remote(gbuf.at[0], rs_in.at[k], rs_s.at[0], rs_r.at[k], up)

    def ag(k):
        return remote(red, fbuf.at[my_chunk], ag_s.at[k], ag_r.at[my_chunk], zpeer(k))

    def ag_arrived(i):
        return remote(red, fbuf.at[i], ag_s.at[0], ag_r.at[i], up)

    def not_mine(f):
        def go(i):
            @pl.when(i * R != z)
            def _():
                f(i)

        return go

    def reduce_factors():
        @pl.when(is_red)
        def _():
            def add(k, total):
                rs_arrived(k).wait_recv()
                return total + rs_in[k].astype(jnp.float32)

            total = lax.fori_loop(1, Z, add, gbuf[my_chunk].astype(jnp.float32))
            red[...] = total.astype(jnp.bfloat16)
            fbuf[my_chunk] = total.astype(jnp.bfloat16)
            loop(Z, lambda k: ag(k).start(), 1)

    def fq(k):
        _, to = quad_of(k)
        return remote(fbuf.at[:, :, pl.ds(0, 128)], fpair.at[k - 1], fq_s.at[k], fq_r.at[k], to)

    fh_sib = remote(fbuf.at[:, :, pl.ds(128, QC)], fsib, fq_s.at[0], fq_r.at[0], sibling)

    def gather_factors():
        loop(NC, not_mine(lambda i: ag_arrived(i).wait_recv()))
        fh_sib.start()
        for k in (1, 2, 3):
            fq(k).start()

    def lf(k):
        n_y = NPL // 2
        i = lax.rem(lax.div(me_pl, 2) + k, n_y)
        to = dev(lax.div(i, NY), lax.rem(i, NY), z, c)
        ref = left_all.at[yl, mp]
        return remote(ref, ref, lf_s.at[k], lf_r.at[k], to)

    def lf_arrived(k):
        n_y = NPL // 2
        i = lax.rem(lax.div(me_pl, 2) + n_y - k, n_y)
        ref = left_all.at[lax.rem(i, 2), lax.div(i, NY) * YH + lax.div(lax.rem(i, NY), 2)]
        return remote(ref, ref, lf_s.at[k], lf_r.at[k], up)

    def left_part():
        total = jnp.zeros((16, T), jnp.float32)
        for k in range(4):
            q = lax.rem(quarter + 4 - k, 4)
            if k:
                fq(k).wait_recv()
            for i in range(NC):
                f = fbuf[i, :, :128] if k == 0 else fpair[k - 1, i]
                kk = pl.ds(pl.multiple_of(q * (D // 4) + i * 128, 128), 128)
                total = total + lax.dot_general(f, tokens[:, kk], NT, preferred_element_type=jnp.float32)
        left_all[yl, mp] = total
        loop(NPL // 2, lambda k: lf(k).start(), 1)

    def multiply(direction, s):
        for a in (0, 1):
            if s == 0:
                sib(0, a, 0).wait_recv()
            elif s <= hops(direction, a):
                sib(direction, a, s).wait_recv()
            elif s == S:
                sib(1 - direction, a, s).wait_recv()
        block = wbuf[at(direction, s)].reshape(4 * WR, H)
        k0, k1 = cols(direction, s, 0), cols(direction, s, 1)
        own = jnp.concatenate([tokens[:, k0], tokens[:, k1]], axis=1)
        acc[0] = acc[0] + jnp.dot(own, block, preferred_element_type=jnp.float32)
        tok(direction, s, 0).wait_recv()
        tok(direction, s, 1).wait_recv()
        other = jnp.concatenate([tok2[:, k0], tok2[:, k1]], axis=1)
        acc[1] = acc[1] + jnp.dot(other, block, preferred_element_type=jnp.float32)

    def advance(direction, a, s):
        if s <= hops(direction, a):
            ring(direction, a, s).wait_recv()
            if s + 1 <= hops(direction, a):
                ring(direction, a, s + 1).start()
            sib(direction, a, s).start()

    acc[...] = jnp.zeros_like(acc)
    for s in range(1, S + 1):
        for direction, a in ((0, 0), (1, 1), (0, 1), (1, 0)):
            advance(direction, a, s)
        if s + 2 <= S:
            tok_start(0, s + 2)
            tok_start(1, s + 2)
        if s == 1:
            pl.semaphore_wait(know.at[1], len(far2))
            tell(know.at[2], far4)
            pick_factors()
        if s == min(2, S):
            pl.semaphore_wait(know.at[2], len(far4))
            loop(NC, not_mine(lambda i: rs(i).start()))
            pair_hg.start()
        if s == min(5, S):
            reduce_factors()
        if s == 2:
            multiply(1, 0)
        elif s > 2:
            multiply(0, s - 2)
            multiply(1, s - 2)
    if S == 1:
        multiply(1, 0)
    else:
        multiply(0, S - 1)
        multiply(1, S - 1)
    gather_factors()
    left_part()
    multiply(0, S)

    pair_hg.wait_recv()
    pair_routes.wait_recv()
    pair_slots.wait_recv()
    for i in (5, 6, 7, 8):
        own[i].wait()
    fh_sib.wait_recv()
    fh_own = fbuf[:, :, 128:].reshape(NC * 16, QC)
    fh_other = fsib[...].reshape(NC * 16, QC)
    fh = jnp.concatenate([jnp.where(c == 0, fh_own, fh_other), jnp.where(c == 0, fh_other, fh_own)], axis=1)
    shift = bias[...]
    rows = 32
    for g in (0, 1):

        def some(i, carry, g=g):
            at_rows = pl.ds(pl.multiple_of(i * rows, rows), rows)
            grads = hg[at_rows, :] if g == 0 else hg2[at_rows, :]
            delta = grads.astype(jnp.float32) * slope(acc[g, at_rows, :] + shift)
            high = delta.astype(jnp.bfloat16)
            dhi[g, at_rows, :] = high
            dlo[g, at_rows, :] = (delta - high.astype(jnp.float32)).astype(jnp.bfloat16)
            return carry

        lax.fori_loop(0, T // rows, some, 0)
    loop(NPL // 2, lambda k: lf_arrived(k).wait_recv(), 1)
    total = jnp.zeros((Z * 4, 128), jnp.float32)
    bits = Z.bit_length()
    n_q = NC * 16 // RANK
    for g in (0, 1):
        right = lax.dot_general(fh, dhi[g], NT, preferred_element_type=jnp.float32)
        right = right + lax.dot_general(fh, dlo[g], NT, preferred_element_type=jnp.float32)
        left = left_all[yl if g == 0 else 1 - yl].reshape(NC * 16, T)
        contrib = (left * right).reshape(n_q, RANK, T).sum(axis=1)
        dest, slot = keys[2 * g], keys[2 * g + 1]
        there = (dest >> 1 & Z - 1) * 4 + (dest >> bits) * 2 + (dest & 1)
        wide = jnp.concatenate([contrib] * (128 // n_q), axis=0)
        slot_of = lax.div(lax.broadcasted_iota(jnp.int32, (128, T), 0), n_q)
        wide = jnp.where(slot_of == slot, wide, 0.0)
        place = lax.broadcasted_iota(jnp.int32, (Z * 4, T), 0)
        named = jnp.where(place == there, 1.0, 0.0).astype(jnp.bfloat16)
        high = wide.astype(jnp.bfloat16)
        rest = wide - high.astype(jnp.float32)
        mid = rest.astype(jnp.bfloat16)
        low = (rest - mid.astype(jnp.float32)).astype(jnp.bfloat16)
        for part in (high, mid, low):
            total = total + lax.dot_general(named, part, NT, preferred_element_type=jnp.float32)
    for i in range(Z):
        terms[i] = total[i * 4 : i * 4 + 4]

    def t1(k):
        return remote(terms.at[lax.rem(z + k, Z)], t1_in.at[k], t1_s.at[k], t1_r.at[k], zpeer(k))

    def t2(k):
        return remote(psum, t2_in.at[k], t2_s.at[k], t2_r.at[k], plane(k))

    loop(Z, lambda k: t1(k).start(), 1)

    def add1(k, total):
        t1(k).wait_recv()
        return total + t1_in[k]

    mine = lax.fori_loop(1, Z, add1, terms[z])
    psum[...] = mine
    loop(NPL, lambda k: t2(k).start(), 1)

    def add2(k, total):
        t2(k).wait_recv()
        return total + t2_in[k]

    mine = lax.fori_loop(1, NPL, add2, mine)
    row = lax.broadcasted_iota(jnp.int32, (4, 128), 0)
    scores = jnp.sum(jnp.where(row == quarter, mine, 0.0), axis=0, keepdims=True)
    for e in range(EX_OUT):
        out[e : e + 1, :] = scores[:, e * n_q : (e + 1) * n_q]

    for cp in (pair_w, pair_routes, pair_slots, pair_hg, fh_sib):
        cp.wait_send()
    for direction in (0, 1):
        for a in (0, 1):
            for s in range(1, hops(direction, a) + 1):
                ring(direction, a, s).wait_send()
                sib(direction, a, s).wait_send()
    for a in (0, 1):
        sib(0, a, 0).wait_send()
    for direction in (0, 1):
        for s in range(1 - direction, S + 1 - direction):
            for h in (0, 1):
                tok(direction, s, h).wait_send()
    for k in (1, 2, 3):
        for cp in quad(k):
            cp.wait_send()
        fq(k).wait_send()
    loop(NC, not_mine(lambda i: rs(i).wait_send()))

    @pl.when(is_red)
    def _():
        loop(Z, lambda k: ag(k).wait_send(), 1)

    loop(NPL // 2, lambda k: lf(k).wait_send(), 1)
    loop(Z, lambda k: t1(k).wait_send(), 1)
    loop(NPL, lambda k: t2(k).wait_send(), 1)


def body(X, YH, Z, tokens, hidden_grad, w_in, b_in, query_in, query_hidden, owners, routes, example_slot):
    T, D = tokens.shape
    M = query_in.shape[0]
    NB = X * YH * 16 // M
    H = w_in.shape[1] // 2
    QC = H // 2
    NC = 2 * NB
    NY, S = 2 * YH, Z // 2
    NPL = X * NY * 2
    bf, f32 = jnp.bfloat16, jnp.float32
    dma = pltpu.SemaphoreType.DMA
    vmem = pl.BlockSpec(memory_space=pltpu.VMEM)
    anywhere = pl.BlockSpec(memory_space=pl.ANY)
    scratch = [
        pltpu.SMEM(owners.shape, jnp.int32),
        pltpu.VMEM((T, D), bf),
        pltpu.VMEM((T, H), bf),
        pltpu.VMEM((1, H), f32),
        pltpu.VMEM((4, 1, T), jnp.int32),
        pltpu.VMEM((Z, 2, 2, w_in.shape[0], H), bf),
        pltpu.VMEM((T, D), bf),
        pltpu.VMEM((2, T, H), f32),
        pltpu.VMEM((T, H), bf),
        pltpu.VMEM((2, T, H), bf),
        pltpu.VMEM((2, T, H), bf),
        pltpu.VMEM((4, 16, D // 4), bf),
        pltpu.VMEM((4, M, QC), bf),
        pltpu.VMEM((NC, 16, 128 + QC), bf),
        pltpu.VMEM((Z, 16, 128 + QC), bf),
        pltpu.VMEM((16, 128 + QC), bf),
        pltpu.VMEM((NC, 16, 128 + QC), bf),
        pltpu.VMEM((NC, 16, QC), bf),
        pltpu.VMEM((3, NC, 16, 128), bf),
        pltpu.VMEM((2, X * YH, 16, T), f32),
        pltpu.VMEM((Z, 4, 128), f32),
        pltpu.VMEM((Z, 4, 128), f32),
        pltpu.VMEM((4, 128), f32),
        pltpu.VMEM((NPL, 4, 128), f32),
    ]
    scratch += [dma((2, 2, S + 1))] * 4 + [dma((2, S + 1, 2))] * 2 + [dma((4,))] * 2
    scratch += [dma((2, 4))] * 2 + [dma((NC,)), dma((Z,)), dma((Z,)), dma((NC,))] + [dma((4,))] * 2
    scratch += [dma((NPL // 2,))] * 2 + [dma((Z,))] * 2 + [dma((NPL,))] * 2 + [dma((9,)), pltpu.SemaphoreType.REGULAR((3,))]
    return pl.pallas_call(
        functools.partial(kernel, X, YH, Z, NB),
        out_shape=jax.ShapeDtypeStruct((EX_OUT, NC * 16 // RANK), f32),
        in_specs=[anywhere] * 9,
        out_specs=vmem,
        scratch_shapes=scratch,
        compiler_params=pltpu.CompilerParams(
            collective_id=0, has_side_effects=True, vmem_limit_bytes=60 * 2**20
        ),
    )(owners, tokens, hidden_grad, w_in, b_in[None], query_in, query_hidden, routes.reshape(1, T), example_slot[None])


def solution(mesh, YH=2):
    Z = mesh.shape["dp"] // 4
    X = mesh.shape["mp"] // YH
    in_specs = (
        P("dp", None), P("dp", "mp"), P("dp", "mp"), P("mp"), P("dp", None), P("dp", "mp"), P(),
        P("dp", None), P("dp"),
    )
    return jax.shard_map(
        functools.partial(body, X, YH, Z), mesh=mesh, in_specs=in_specs, out_specs=P("dp", None), check_vma=False
    )
```

```python
import functools

import jax
import jax.numpy as jnp
from jax import lax
from jax.experimental import pallas as pl
from jax.experimental.pallas import tpu as pltpu
from jax.sharding import PartitionSpec as P

MESH = pl.DeviceIdType.MESH
RANK = 8
EX_OUT = 8
NT = (((1,), (1,)), ((), ()))


def slope(pre):
    cdf = 0.5 * (1.0 + lax.erf(pre * 0.7071067811865476))
    dens = jnp.exp(-0.5 * pre * pre) * 0.3989422804014327
    return cdf + pre * dens


def kernel(
    X, YH, Z, NB,
    owners_in, tok_in, hg_in, w, bias_in, qi, qh, routes, slots, out,
    owners, tokens, hg, bias, keys,
    wbuf, tok2, acc, hg2, dhi, dlo,
    qi_raw, qh_raw, gbuf, rs_in, red, fbuf, fsib, fpair, left_all,
    terms, t1_in, psum, t2_in,
    ring_s, ring_r, sib_s, sib_r, tok_s, tok_r, pair_s, pair_r, quad_s, quad_r,
    rs_s, rs_r, ag_s, ag_r, fq_s, fq_r, lf_s, lf_r, t1_s, t1_r, t2_s, t2_r, loc_s,
):
    NY, S, NC = 2 * YH, Z // 2, 2 * NB
    T, D = tok_in.shape
    WR, H = w.shape[0], w.shape[1] // 2
    QC = H // 2
    NPL = X * NY * 2
    R = Z // NC
    dp, mp = lax.axis_index("dp"), lax.axis_index("mp")
    c = lax.rem(dp, 2)
    z = lax.rem(lax.div(dp, 2), Z)
    yl = lax.div(dp, 2 * Z)
    yh = lax.rem(mp, YH)
    x = lax.div(mp, YH)
    y = yh * 2 + yl
    me_pl = (x * NY + y) * 2 + c
    quarter = yl * 2 + c

    def dev(x_, y_, z_, c_):
        return ((lax.rem(y_, 2) * Z + z_) * 2 + c_, x_ * YH + lax.div(y_, 2))

    def zpeer(k):
        return dev(x, y, lax.rem(z + k, Z), c)

    def plane(k):
        i = lax.rem(me_pl + k, NPL)
        return dev(lax.div(i, NY * 2), lax.rem(lax.div(i, 2), NY), z, lax.rem(i, 2))

    def remote(src, dst, send, recv, to):
        return pltpu.make_async_remote_copy(
            src_ref=src, dst_ref=dst, send_sem=send, recv_sem=recv,
            device_id=to, device_id_type=MESH,
        )

    def loop(n, f, start=0):
        def step(i, carry):
            f(i)
            return carry

        lax.fori_loop(start, n, step, 0)

    b_mine, h_mine = lax.div(mp, 2), lax.rem(mp, 2)
    qrows = pl.ds(pl.multiple_of(h_mine * 16, 16), 16)

    def half(i):
        return pl.ds(pl.multiple_of(i * H, H), H)

    locals_ = [
        (w.at[:, half(yl)], wbuf.at[z, yl, c]),
        (qi.at[qrows, pl.ds(pl.multiple_of(quarter * (D // 4), 128), D // 4)], qi_raw.at[0]),
        (qh.at[:, pl.ds(pl.multiple_of(quarter * QC, 128), QC)], qh_raw.at[0]),
        (owners_in, owners),
        (tok_in, tokens),
        (hg_in.at[:, half(yl)], hg),
        (bias_in.at[:, half(yl)], bias),
        (routes, keys.at[0]),
        (slots, keys.at[1]),
    ]
    own = [pltpu.make_async_copy(src, dst, loc_s.at[i]) for i, (src, dst) in enumerate(locals_)]
    for cp in own:
        cp.start()

    barrier = pltpu.get_barrier_semaphore()
    loop(Z, lambda k: pl.semaphore_signal(barrier, inc=1, device_id=zpeer(k), device_id_type=MESH), 1)
    loop(NPL, lambda k: pl.semaphore_signal(barrier, inc=1, device_id=plane(k), device_id_type=MESH), 1)
    pl.semaphore_wait(barrier, Z - 1 + NPL - 1)

    sibling = dev(x, y, z, 1 - c)
    partner = dev(x, yh * 2 + 1 - yl, z, c)
    up, down = zpeer(1), zpeer(Z - 1)
    y_up = dev(x, lax.rem(y + 1, NY), z, c)
    y_down = dev(x, lax.rem(y + NY - 1, NY), z, c)

    pair_w = remote(w.at[:, half(1 - yl)], wbuf.at[z, yl, c], pair_s.at[0], pair_r.at[0], partner)
    pair_w.start()
    own[0].wait()

    def at(direction, s):
        return lax.rem(z + (Z - s if direction == 0 else s), Z)

    def ring(direction, a, s):
        ref = wbuf.at[at(direction, s - 1), a, c]
        return remote(
            ref, ref, ring_s.at[direction, a, s], ring_r.at[direction, a, s], (up, down)[direction]
        )

    def sib(direction, a, s):
        ref = wbuf.at[at(direction, s), a, c]
        return remote(ref, ref, sib_s.at[direction, a, s], sib_r.at[direction, a, s], sibling)

    def hops(direction, a):
        return S if direction == a else S - 1

    def cols(direction, s, h):
        return pl.ds(pl.multiple_of(h * (D // 2) + at(direction, s) * 2 * WR, 2 * WR), 2 * WR)

    def tok(direction, s, h):
        k = cols(direction, s, h)
        return remote(
            tokens.at[:, k], tok2.at[:, k], tok_s.at[direction, s, h], tok_r.at[direction, s, h],
            (y_up, y_down)[direction],
        )

    def tok_start(direction, s):
        if (1 if direction == 0 else 0) <= s <= (S if direction == 0 else S - 1):
            tok(direction, s, 0).start()
            tok(direction, s, 1).start()

    def first(a):
        ring(0, a, 1).start()
        ring(1, a, 1).start()
        sib(0, a, 0).start()

    first(yl)

    def quad_of(k):
        q = lax.rem(quarter + k, 4)
        return q, dev(x, yh * 2 + lax.div(q, 2), z, lax.rem(q, 2))

    def quad(k):
        q, to = quad_of(k)
        a = remote(
            qi.at[qrows, pl.ds(pl.multiple_of(q * (D // 4), 128), D // 4)], qi_raw.at[k],
            quad_s.at[0, k], quad_r.at[0, k], to,
        )
        b = remote(
            qh.at[:, pl.ds(pl.multiple_of(q * QC, 128), QC)], qh_raw.at[k],
            quad_s.at[1, k], quad_r.at[1, k], to,
        )
        return a, b

    for k in (1, 2, 3):
        for cp in quad(k):
            cp.start()
    pair_routes = remote(routes, keys.at[2], pair_s.at[1], pair_r.at[1], partner)
    pair_routes.start()
    pair_slots = remote(slots, keys.at[3], pair_s.at[3], pair_r.at[3], partner)
    pair_slots.start()

    pair_w.wait_recv()
    first(1 - yl)
    own[4].wait()
    for s in (0, 1, 2):
        tok_start(0, s)
        tok_start(1, s)
    pair_hg = remote(hg_in.at[:, half(1 - yl)], hg2, pair_s.at[2], pair_r.at[2], partner)

    for k in (1, 2, 3):
        for cp in quad(k):
            cp.wait_recv()
    for i in (1, 2, 3):
        own[i].wait()
    srcs = []
    for k in range(4):
        q = lax.rem(quarter + 4 - k, 4)
        srcs.append((lax.div(q, 2) * Z + z) * 2 + lax.rem(q, 2))

    def pick(b, k):
        return jnp.where(owners[b] == srcs[k], 1.0, 0.0).astype(jnp.float32)

    for i in range(NC):
        b, h = i // 2, i % 2
        gi = sum(pick(b_mine, k) * qi_raw[k, :, i * 128 : (i + 1) * 128].astype(jnp.float32) for k in range(4))
        gh = sum(pick(b, k) * qh_raw[k, h * 16 : (h + 1) * 16].astype(jnp.float32) for k in range(4))
        gbuf[i, :, :128] = gi.astype(jnp.bfloat16)
        gbuf[i, :, 128:] = gh.astype(jnp.bfloat16)

    is_red = lax.rem(z, R) == 0
    my_chunk = lax.div(z, R)

    def rs(i):
        k = lax.rem(z + Z - i * R, Z)
        return remote(gbuf.at[i], rs_in.at[k], rs_s.at[i], rs_r.at[k], dev(x, y, i * R, c))

    def rs_arrived(k):
        return remote(gbuf.at[0], rs_in.at[k], rs_s.at[0], rs_r.at[k], up)

    def ag(k):
        return remote(red, fbuf.at[my_chunk], ag_s.at[k], ag_r.at[my_chunk], zpeer(k))

    def ag_arrived(i):
        return remote(red, fbuf.at[i], ag_s.at[0], ag_r.at[i], up)

    def not_mine(f):
        def go(i):
            @pl.when(i * R != z)
            def _():
                f(i)

        return go

    loop(NC, not_mine(lambda i: rs(i).start()))

    def reduce_factors():
        @pl.when(is_red)
        def _():
            def add(k, total):
                rs_arrived(k).wait_recv()
                return total + rs_in[k].astype(jnp.float32)

            total = lax.fori_loop(1, Z, add, gbuf[my_chunk].astype(jnp.float32))
            red[...] = total.astype(jnp.bfloat16)
            fbuf[my_chunk] = total.astype(jnp.bfloat16)
            loop(Z, lambda k: ag(k).start(), 1)

    def fq(k):
        _, to = quad_of(k)
        return remote(fbuf.at[:, :, pl.ds(0, 128)], fpair.at[k - 1], fq_s.at[k], fq_r.at[k], to)

    fh_sib = remote(fbuf.at[:, :, pl.ds(128, QC)], fsib, fq_s.at[0], fq_r.at[0], sibling)

    def gather_factors():
        loop(NC, not_mine(lambda i: ag_arrived(i).wait_recv()))
        fh_sib.start()
        for k in (1, 2, 3):
            fq(k).start()

    def lf(k):
        n_y = NPL // 2
        i = lax.rem(lax.div(me_pl, 2) + k, n_y)
        to = dev(lax.div(i, NY), lax.rem(i, NY), z, c)
        ref = left_all.at[yl, mp]
        return remote(ref, ref, lf_s.at[k], lf_r.at[k], to)

    def lf_arrived(k):
        n_y = NPL // 2
        i = lax.rem(lax.div(me_pl, 2) + n_y - k, n_y)
        ref = left_all.at[lax.rem(i, 2), lax.div(i, NY) * YH + lax.div(lax.rem(i, NY), 2)]
        return remote(ref, ref, lf_s.at[k], lf_r.at[k], up)

    def left_part():
        total = jnp.zeros((16, T), jnp.float32)
        for k in range(4):
            q = lax.rem(quarter + 4 - k, 4)
            if k:
                fq(k).wait_recv()
            for i in range(NC):
                f = fbuf[i, :, :128] if k == 0 else fpair[k - 1, i]
                kk = pl.ds(pl.multiple_of(q * (D // 4) + i * 128, 128), 128)
                total = total + lax.dot_general(f, tokens[:, kk], NT, preferred_element_type=jnp.float32)
        left_all[yl, mp] = total
        loop(NPL // 2, lambda k: lf(k).start(), 1)

    def multiply(direction, s):
        for a in (0, 1):
            if s == 0:
                sib(0, a, 0).wait_recv()
            elif s <= hops(direction, a):
                sib(direction, a, s).wait_recv()
            elif s == S:
                sib(1 - direction, a, s).wait_recv()
        block = wbuf[at(direction, s)].reshape(4 * WR, H)
        k0, k1 = cols(direction, s, 0), cols(direction, s, 1)
        own = jnp.concatenate([tokens[:, k0], tokens[:, k1]], axis=1)
        acc[0] = acc[0] + jnp.dot(own, block, preferred_element_type=jnp.float32)
        tok(direction, s, 0).wait_recv()
        tok(direction, s, 1).wait_recv()
        other = jnp.concatenate([tok2[:, k0], tok2[:, k1]], axis=1)
        acc[1] = acc[1] + jnp.dot(other, block, preferred_element_type=jnp.float32)

    def advance(direction, a, s):
        if s <= hops(direction, a):
            ring(direction, a, s).wait_recv()
            if s + 1 <= hops(direction, a):
                ring(direction, a, s + 1).start()
            sib(direction, a, s).start()

    acc[...] = jnp.zeros_like(acc)
    for s in range(1, S + 1):
        for direction, a in ((0, 0), (1, 1), (0, 1), (1, 0)):
            advance(direction, a, s)
        if s + 2 <= S:
            tok_start(0, s + 2)
            tok_start(1, s + 2)
        if s == min(2, S):
            pair_hg.start()
        if s == min(3, S):
            reduce_factors()
        if s == min(5, S):
            gather_factors()
        if s == min(6, S):
            left_part()
        if s == 1:
            multiply(1, 0)
        else:
            multiply(0, s - 1)
            multiply(1, s - 1)
    multiply(0, S)

    pair_hg.wait_recv()
    pair_routes.wait_recv()
    pair_slots.wait_recv()
    for i in (5, 6, 7, 8):
        own[i].wait()
    fh_sib.wait_recv()
    fh_own = fbuf[:, :, 128:].reshape(NC * 16, QC)
    fh_other = fsib[...].reshape(NC * 16, QC)
    fh = jnp.concatenate([jnp.where(c == 0, fh_own, fh_other), jnp.where(c == 0, fh_other, fh_own)], axis=1)
    shift = bias[...]
    rows = 32
    for g in (0, 1):

        def some(i, carry, g=g):
            at_rows = pl.ds(pl.multiple_of(i * rows, rows), rows)
            grads = hg[at_rows, :] if g == 0 else hg2[at_rows, :]
            delta = grads.astype(jnp.float32) * slope(acc[g, at_rows, :] + shift)
            high = delta.astype(jnp.bfloat16)
            dhi[g, at_rows, :] = high
            dlo[g, at_rows, :] = (delta - high.astype(jnp.float32)).astype(jnp.bfloat16)
            return carry

        lax.fori_loop(0, T // rows, some, 0)
    loop(NPL // 2, lambda k: lf_arrived(k).wait_recv(), 1)
    total = jnp.zeros((Z * 4, 128), jnp.float32)
    bits = Z.bit_length()
    n_q = NC * 16 // RANK
    for g in (0, 1):
        right = lax.dot_general(fh, dhi[g], NT, preferred_element_type=jnp.float32)
        right = right + lax.dot_general(fh, dlo[g], NT, preferred_element_type=jnp.float32)
        left = left_all[yl if g == 0 else 1 - yl].reshape(NC * 16, T)
        contrib = (left * right).reshape(n_q, RANK, T).sum(axis=1)
        dest, slot = keys[2 * g], keys[2 * g + 1]
        there = (dest >> 1 & Z - 1) * 4 + (dest >> bits) * 2 + (dest & 1)
        wide = jnp.concatenate([contrib] * (128 // n_q), axis=0)
        slot_of = lax.div(lax.broadcasted_iota(jnp.int32, (128, T), 0), n_q)
        wide = jnp.where(slot_of == slot, wide, 0.0)
        place = lax.broadcasted_iota(jnp.int32, (Z * 4, T), 0)
        named = jnp.where(place == there, 1.0, 0.0).astype(jnp.bfloat16)
        high = wide.astype(jnp.bfloat16)
        rest = wide - high.astype(jnp.float32)
        mid = rest.astype(jnp.bfloat16)
        low = (rest - mid.astype(jnp.float32)).astype(jnp.bfloat16)
        for part in (high, mid, low):
            total = total + lax.dot_general(named, part, NT, preferred_element_type=jnp.float32)
    for i in range(Z):
        terms[i] = total[i * 4 : i * 4 + 4]

    def t1(k):
        return remote(terms.at[lax.rem(z + k, Z)], t1_in.at[k], t1_s.at[k], t1_r.at[k], zpeer(k))

    def t2(k):
        return remote(psum, t2_in.at[k], t2_s.at[k], t2_r.at[k], plane(k))

    loop(Z, lambda k: t1(k).start(), 1)

    def add1(k, total):
        t1(k).wait_recv()
        return total + t1_in[k]

    mine = lax.fori_loop(1, Z, add1, terms[z])
    psum[...] = mine
    loop(NPL, lambda k: t2(k).start(), 1)

    def add2(k, total):
        t2(k).wait_recv()
        return total + t2_in[k]

    mine = lax.fori_loop(1, NPL, add2, mine)
    row = lax.broadcasted_iota(jnp.int32, (4, 128), 0)
    scores = jnp.sum(jnp.where(row == quarter, mine, 0.0), axis=0, keepdims=True)
    for e in range(EX_OUT):
        out[e : e + 1, :] = scores[:, e * n_q : (e + 1) * n_q]

    for cp in (pair_w, pair_routes, pair_slots, pair_hg, fh_sib):
        cp.wait_send()
    for direction in (0, 1):
        for a in (0, 1):
            for s in range(1, hops(direction, a) + 1):
                ring(direction, a, s).wait_send()
                sib(direction, a, s).wait_send()
    for a in (0, 1):
        sib(0, a, 0).wait_send()
    for direction in (0, 1):
        for s in range(1 - direction, S + 1 - direction):
            for h in (0, 1):
                tok(direction, s, h).wait_send()
    for k in (1, 2, 3):
        for cp in quad(k):
            cp.wait_send()
        fq(k).wait_send()
    loop(NC, not_mine(lambda i: rs(i).wait_send()))

    @pl.when(is_red)
    def _():
        loop(Z, lambda k: ag(k).wait_send(), 1)

    loop(NPL // 2, lambda k: lf(k).wait_send(), 1)
    loop(Z, lambda k: t1(k).wait_send(), 1)
    loop(NPL, lambda k: t2(k).wait_send(), 1)


def body(X, YH, Z, tokens, hidden_grad, w_in, b_in, query_in, query_hidden, owners, routes, example_slot):
    T, D = tokens.shape
    M = query_in.shape[0]
    NB = X * YH * 16 // M
    H = w_in.shape[1] // 2
    QC = H // 2
    NC = 2 * NB
    NY, S = 2 * YH, Z // 2
    NPL = X * NY * 2
    bf, f32 = jnp.bfloat16, jnp.float32
    dma = pltpu.SemaphoreType.DMA
    vmem = pl.BlockSpec(memory_space=pltpu.VMEM)
    anywhere = pl.BlockSpec(memory_space=pl.ANY)
    scratch = [
        pltpu.SMEM(owners.shape, jnp.int32),
        pltpu.VMEM((T, D), bf),
        pltpu.VMEM((T, H), bf),
        pltpu.VMEM((1, H), f32),
        pltpu.VMEM((4, 1, T), jnp.int32),
        pltpu.VMEM((Z, 2, 2, w_in.shape[0], H), bf),
        pltpu.VMEM((T, D), bf),
        pltpu.VMEM((2, T, H), f32),
        pltpu.VMEM((T, H), bf),
        pltpu.VMEM((2, T, H), bf),
        pltpu.VMEM((2, T, H), bf),
        pltpu.VMEM((4, 16, D // 4), bf),
        pltpu.VMEM((4, M, QC), bf),
        pltpu.VMEM((NC, 16, 128 + QC), bf),
        pltpu.VMEM((Z, 16, 128 + QC), bf),
        pltpu.VMEM((16, 128 + QC), bf),
        pltpu.VMEM((NC, 16, 128 + QC), bf),
        pltpu.VMEM((NC, 16, QC), bf),
        pltpu.VMEM((3, NC, 16, 128), bf),
        pltpu.VMEM((2, X * YH, 16, T), f32),
        pltpu.VMEM((Z, 4, 128), f32),
        pltpu.VMEM((Z, 4, 128), f32),
        pltpu.VMEM((4, 128), f32),
        pltpu.VMEM((NPL, 4, 128), f32),
    ]
    scratch += [dma((2, 2, S + 1))] * 4 + [dma((2, S + 1, 2))] * 2 + [dma((4,))] * 2
    scratch += [dma((2, 4))] * 2 + [dma((NC,)), dma((Z,)), dma((Z,)), dma((NC,))] + [dma((4,))] * 2
    scratch += [dma((NPL // 2,))] * 2 + [dma((Z,))] * 2 + [dma((NPL,))] * 2 + [dma((9,))]
    return pl.pallas_call(
        functools.partial(kernel, X, YH, Z, NB),
        out_shape=jax.ShapeDtypeStruct((EX_OUT, NC * 16 // RANK), f32),
        in_specs=[anywhere] * 9,
        out_specs=vmem,
        scratch_shapes=scratch,
        compiler_params=pltpu.CompilerParams(
            collective_id=0, has_side_effects=True, vmem_limit_bytes=60 * 2**20
        ),
    )(owners, tokens, hidden_grad, w_in, b_in[None], query_in, query_hidden, routes.reshape(1, T), example_slot[None])


def solution(mesh, YH=2):
    Z = mesh.shape["dp"] // 4
    X = mesh.shape["mp"] // YH
    in_specs = (
        P("dp", None), P("dp", "mp"), P("dp", "mp"), P("mp"), P("dp", None), P("dp", "mp"), P(),
        P("dp", None), P("dp"),
    )
    return jax.shard_map(
        functools.partial(body, X, YH, Z), mesh=mesh, in_specs=in_specs, out_specs=P("dp", None), check_vma=False
    )
```

```python
import functools

import jax
import jax.numpy as jnp
from jax import lax
from jax.experimental import pallas as pl
from jax.experimental.pallas import tpu as pltpu
from jax.sharding import PartitionSpec as P

MESH = pl.DeviceIdType.MESH
RANK = 8
EX_OUT = 8
NT = (((1,), (1,)), ((), ()))


def slope(pre):
    cdf = 0.5 * (1.0 + lax.erf(pre * 0.7071067811865476))
    dens = jnp.exp(-0.5 * pre * pre) * 0.3989422804014327
    return cdf + pre * dens


def kernel(
    X, YH, Z, NB,
    owners_in, tok_in, hg_in, w, bias_in, qi, qh, routes, slots, out,
    owners, tokens, hg, bias, keys,
    wbuf, tok2, acc, hg2, dhi, dlo,
    qi_raw, qh_raw, gbuf, st1, hbuf, st2, fbuf, fsib, fpair, left_all,
    terms, t1_in, psum, t2_in,
    ring_s, ring_r, sib_s, sib_r, tok_s, tok_r, pair_s, pair_r, quad_s, quad_r,
    r1_s, r1_r, r2_s, r2_r, aa_s, aa_r, ab_s, ab_r, fq_s, fq_r, lf_s, lf_r, t1_s, t1_r, t2_s, t2_r, loc_s,
):
    NY, S, NC = 2 * YH, Z // 2, 2 * NB
    T, D = tok_in.shape
    WR, H = w.shape[0], w.shape[1] // 2
    QC = H // 2
    NPL = X * NY * 2
    dp, mp = lax.axis_index("dp"), lax.axis_index("mp")
    c = lax.rem(dp, 2)
    z = lax.rem(lax.div(dp, 2), Z)
    yl = lax.div(dp, 2 * Z)
    yh = lax.rem(mp, YH)
    x = lax.div(mp, YH)
    y = yh * 2 + yl
    me_pl = (x * NY + y) * 2 + c
    quarter = yl * 2 + c

    def dev(x_, y_, z_, c_):
        return ((lax.rem(y_, 2) * Z + z_) * 2 + c_, x_ * YH + lax.div(y_, 2))

    def zpeer(k):
        return dev(x, y, lax.rem(z + k, Z), c)

    def plane(k):
        i = lax.rem(me_pl + k, NPL)
        return dev(lax.div(i, NY * 2), lax.rem(lax.div(i, 2), NY), z, lax.rem(i, 2))

    def remote(src, dst, send, recv, to):
        return pltpu.make_async_remote_copy(
            src_ref=src, dst_ref=dst, send_sem=send, recv_sem=recv,
            device_id=to, device_id_type=MESH,
        )

    def loop(n, f, start=0):
        def step(i, carry):
            f(i)
            return carry

        lax.fori_loop(start, n, step, 0)

    b_mine, h_mine = lax.div(mp, 2), lax.rem(mp, 2)
    qrows = pl.ds(pl.multiple_of(h_mine * 16, 16), 16)

    def half(i):
        return pl.ds(pl.multiple_of(i * H, H), H)

    locals_ = [
        (w.at[:, half(yl)], wbuf.at[z, yl, c]),
        (qi.at[qrows, pl.ds(pl.multiple_of(quarter * (D // 4), 128), D // 4)], qi_raw.at[0]),
        (qh.at[:, pl.ds(pl.multiple_of(quarter * QC, 128), QC)], qh_raw.at[0]),
        (owners_in, owners),
        (tok_in, tokens),
        (hg_in.at[:, half(yl)], hg),
        (bias_in.at[:, half(yl)], bias),
        (routes, keys.at[0]),
        (slots, keys.at[1]),
    ]
    own = [pltpu.make_async_copy(src, dst, loc_s.at[i]) for i, (src, dst) in enumerate(locals_)]
    for cp in own:
        cp.start()

    barrier = pltpu.get_barrier_semaphore()
    loop(Z, lambda k: pl.semaphore_signal(barrier, inc=1, device_id=zpeer(k), device_id_type=MESH), 1)
    loop(NPL, lambda k: pl.semaphore_signal(barrier, inc=1, device_id=plane(k), device_id_type=MESH), 1)
    pl.semaphore_wait(barrier, Z - 1 + NPL - 1)

    sibling = dev(x, y, z, 1 - c)
    partner = dev(x, yh * 2 + 1 - yl, z, c)
    up, down = zpeer(1), zpeer(Z - 1)
    y_up = dev(x, lax.rem(y + 1, NY), z, c)
    y_down = dev(x, lax.rem(y + NY - 1, NY), z, c)

    pair_w = remote(w.at[:, half(1 - yl)], wbuf.at[z, yl, c], pair_s.at[0], pair_r.at[0], partner)
    pair_w.start()
    own[0].wait()

    def at(direction, s):
        return lax.rem(z + (Z - s if direction == 0 else s), Z)

    def ring(direction, a, s):
        ref = wbuf.at[at(direction, s - 1), a, c]
        return remote(
            ref, ref, ring_s.at[direction, a, s], ring_r.at[direction, a, s], (up, down)[direction]
        )

    def sib(direction, a, s):
        ref = wbuf.at[at(direction, s), a, c]
        return remote(ref, ref, sib_s.at[direction, a, s], sib_r.at[direction, a, s], sibling)

    def hops(direction, a):
        return S if direction == a else S - 1

    def cols(direction, s, h):
        return pl.ds(pl.multiple_of(h * (D // 2) + at(direction, s) * 2 * WR, 2 * WR), 2 * WR)

    def tok(direction, s, h):
        k = cols(direction, s, h)
        return remote(
            tokens.at[:, k], tok2.at[:, k], tok_s.at[direction, s, h], tok_r.at[direction, s, h],
            (y_up, y_down)[direction],
        )

    def tok_start(direction, s):
        if (1 if direction == 0 else 0) <= s <= (S if direction == 0 else S - 1):
            tok(direction, s, 0).start()
            tok(direction, s, 1).start()

    def first(a):
        ring(0, a, 1).start()
        ring(1, a, 1).start()
        sib(0, a, 0).start()

    first(yl)

    def quad_of(k):
        q = lax.rem(quarter + k, 4)
        return q, dev(x, yh * 2 + lax.div(q, 2), z, lax.rem(q, 2))

    def quad(k):
        q, to = quad_of(k)
        a = remote(
            qi.at[qrows, pl.ds(pl.multiple_of(q * (D // 4), 128), D // 4)], qi_raw.at[k],
            quad_s.at[0, k], quad_r.at[0, k], to,
        )
        b = remote(
            qh.at[:, pl.ds(pl.multiple_of(q * QC, 128), QC)], qh_raw.at[k],
            quad_s.at[1, k], quad_r.at[1, k], to,
        )
        return a, b

    for k in (1, 2, 3):
        for cp in quad(k):
            cp.start()
    pair_routes = remote(routes, keys.at[2], pair_s.at[1], pair_r.at[1], partner)
    pair_routes.start()
    pair_slots = remote(slots, keys.at[3], pair_s.at[3], pair_r.at[3], partner)
    pair_slots.start()

    pair_w.wait_recv()
    first(1 - yl)
    own[4].wait()
    for s in (0, 1, 2):
        tok_start(0, s)
        tok_start(1, s)
    pair_hg = remote(hg_in.at[:, half(1 - yl)], hg2, pair_s.at[2], pair_r.at[2], partner)


    def pick_factors():
        for k in (1, 2, 3):
            for cp in quad(k):
                cp.wait_recv()
        for i in (1, 2, 3):
            own[i].wait()
        srcs = []
        for k in range(4):
            q = lax.rem(quarter + 4 - k, 4)
            srcs.append((lax.div(q, 2) * Z + z) * 2 + lax.rem(q, 2))

        def pick(b, k):
            return jnp.where(owners[b] == srcs[k], 1.0, 0.0).astype(jnp.float32)

        for i in range(NC):
            b, h = i // 2, i % 2
            gi = sum(pick(b_mine, k) * qi_raw[k, :, i * 128 : (i + 1) * 128].astype(jnp.float32) for k in range(4))
            gh = sum(pick(b, k) * qh_raw[k, h * 16 : (h + 1) * 16].astype(jnp.float32) for k in range(4))
            gbuf[i % 2, i // 2, :, :128] = gi.astype(jnp.bfloat16)
            gbuf[i % 2, i // 2, :, 128:] = gh.astype(jnp.bfloat16)

    NH = Z // 4
    even = lax.rem(z, 2) == 0
    group, u0 = lax.rem(lax.div(z, 2), 2), lax.div(z, 4)

    def to_head(n):
        src = gbuf.at[group if n == 0 else 1 - group]
        return remote(src, st1.at[n], r1_s.at[n], r1_r.at[n], zpeer((Z - 1, Z - 2, 1)[n]))

    def between_heads(m):
        return remote(hbuf.at[lax.rem(u0 + m, NH)], st2.at[m], r2_s.at[m], r2_r.at[m], zpeer(4 * m))

    def share(m):
        ref = fbuf.at[group, u0]
        return remote(ref, ref, aa_s.at[m], aa_r.at[m], zpeer(4 * m))

    def share_arrived(m):
        ref = fbuf.at[group, lax.rem(u0 + NH - m, NH)]
        return remote(ref, ref, aa_s.at[m], aa_r.at[m], up)

    def from_head(n):
        ref = fbuf.at[group]
        return remote(ref, ref, ab_s.at[n], ab_r.at[n], zpeer((Z - 1, Z - 2, 1)[n]))

    def head_arrived(n):
        ref = fbuf.at[group if n == 2 else 1 - group]
        return remote(ref, ref, ab_s.at[n], ab_r.at[n], up)

    def when_even(f):
        pl.when(even)(f)

    def when_odd(f):
        pl.when(jnp.logical_not(even))(f)

    def stage1():
        @when_odd
        def _():
            to_head(0).start()
            to_head(2).start()

        @when_even
        def _():
            to_head(1).start()

    def stage2():
        @when_even
        def _():
            total = gbuf[group].astype(jnp.float32)
            for n in range(3):
                to_head(n).wait_recv()
                total = total + st1[n].astype(jnp.float32)
            hbuf[...] = total.astype(jnp.bfloat16)
            for m in range(1, NH):
                between_heads(m).start()

    def stage3():
        @when_even
        def _():
            total = hbuf[u0].astype(jnp.float32)
            for m in range(1, NH):
                between_heads(m).wait_recv()
                total = total + st2[m].astype(jnp.float32)
            fbuf[group, u0] = total.astype(jnp.bfloat16)
            for m in range(1, NH):
                share(m).start()

    def stage4():
        @when_even
        def _():
            for m in range(1, NH):
                share_arrived(m).wait_recv()
            for n in range(3):
                from_head(n).start()

    def stages_sent():
        @when_odd
        def _():
            to_head(0).wait_send()
            to_head(2).wait_send()

        @when_even
        def _():
            to_head(1).wait_send()
            for m in range(1, NH):
                between_heads(m).wait_send()
                share(m).wait_send()
            for n in range(3):
                from_head(n).wait_send()

    def fq(k):
        _, to = quad_of(k)
        return remote(fbuf.at[:, :, :, pl.ds(0, 128)], fpair.at[k - 1], fq_s.at[k], fq_r.at[k], to)

    fh_sib = remote(fbuf.at[:, :, :, pl.ds(128, QC)], fsib, fq_s.at[0], fq_r.at[0], sibling)

    def gather_factors():
        @when_odd
        def _():
            head_arrived(0).wait_recv()
            head_arrived(2).wait_recv()

        @when_even
        def _():
            head_arrived(1).wait_recv()

        fh_sib.start()
        for k in (1, 2, 3):
            fq(k).start()

    def lf(k):
        n_y = NPL // 2
        i = lax.rem(lax.div(me_pl, 2) + k, n_y)
        to = dev(lax.div(i, NY), lax.rem(i, NY), z, c)
        ref = left_all.at[yl, mp]
        return remote(ref, ref, lf_s.at[k], lf_r.at[k], to)

    def lf_arrived(k):
        n_y = NPL // 2
        i = lax.rem(lax.div(me_pl, 2) + n_y - k, n_y)
        ref = left_all.at[lax.rem(i, 2), lax.div(i, NY) * YH + lax.div(lax.rem(i, NY), 2)]
        return remote(ref, ref, lf_s.at[k], lf_r.at[k], up)

    def left_part():
        total = jnp.zeros((16, T), jnp.float32)
        for k in range(4):
            q = lax.rem(quarter + 4 - k, 4)
            if k:
                fq(k).wait_recv()
            f = jnp.concatenate([fbuf[i % 2, i // 2, :, :128] if k == 0 else fpair[k - 1, i % 2, i // 2] for i in range(NC)], axis=1)
            kk = pl.ds(pl.multiple_of(q * (D // 4), D // 4), D // 4)
            total = total + lax.dot_general(f, tokens[:, kk], NT, preferred_element_type=jnp.float32)
        left_all[yl, mp] = total
        loop(NPL // 2, lambda k: lf(k).start(), 1)

    def multiply(direction, s):
        for a in (0, 1):
            if s == 0:
                sib(0, a, 0).wait_recv()
            elif s <= hops(direction, a):
                sib(direction, a, s).wait_recv()
            elif s == S:
                sib(1 - direction, a, s).wait_recv()
        block = wbuf[at(direction, s)].reshape(4 * WR, H)
        k0, k1 = cols(direction, s, 0), cols(direction, s, 1)
        own = jnp.concatenate([tokens[:, k0], tokens[:, k1]], axis=1)
        acc[0] = acc[0] + jnp.dot(own, block, preferred_element_type=jnp.float32)
        tok(direction, s, 0).wait_recv()
        tok(direction, s, 1).wait_recv()
        other = jnp.concatenate([tok2[:, k0], tok2[:, k1]], axis=1)
        acc[1] = acc[1] + jnp.dot(other, block, preferred_element_type=jnp.float32)

    def advance(direction, a, s):
        if s <= hops(direction, a):
            ring(direction, a, s).wait_recv()
            if s + 1 <= hops(direction, a):
                ring(direction, a, s + 1).start()
            sib(direction, a, s).start()

    pick_factors()
    stage1()
    acc[...] = jnp.zeros_like(acc)
    for s in range(1, S + 1):
        for direction, a in ((0, 0), (1, 1), (0, 1), (1, 0)):
            advance(direction, a, s)
        if s + 2 <= S:
            tok_start(0, s + 2)
            tok_start(1, s + 2)
        if s == 1:
            stage2()
        if s == min(2, S):
            pair_hg.start()
        if s == min(3, S):
            stage3()
        if s == min(4, S):
            stage4()
        if s == min(5, S):
            gather_factors()
        if s == min(6, S):
            left_part()
        if s == 2:
            multiply(1, 0)
        elif s > 2:
            multiply(0, s - 2)
            multiply(1, s - 2)
    if S == 1:
        multiply(1, 0)
    else:
        multiply(0, S - 1)
        multiply(1, S - 1)
    multiply(0, S)

    pair_hg.wait_recv()
    pair_routes.wait_recv()
    pair_slots.wait_recv()
    for i in (5, 6, 7, 8):
        own[i].wait()
    fh_sib.wait_recv()
    fh_own = jnp.concatenate([fbuf[i % 2, i // 2, :, 128:] for i in range(NC)], axis=0)
    fh_other = jnp.concatenate([fsib[i % 2, i // 2] for i in range(NC)], axis=0)
    fh = jnp.concatenate([jnp.where(c == 0, fh_own, fh_other), jnp.where(c == 0, fh_other, fh_own)], axis=1)
    shift = bias[...]
    rows = 32
    for g in (0, 1):

        def some(i, carry, g=g):
            at_rows = pl.ds(pl.multiple_of(i * rows, rows), rows)
            grads = hg[at_rows, :] if g == 0 else hg2[at_rows, :]
            delta = grads.astype(jnp.float32) * slope(acc[g, at_rows, :] + shift)
            high = delta.astype(jnp.bfloat16)
            dhi[g, at_rows, :] = high
            dlo[g, at_rows, :] = (delta - high.astype(jnp.float32)).astype(jnp.bfloat16)
            return carry

        lax.fori_loop(0, T // rows, some, 0)
    loop(NPL // 2, lambda k: lf_arrived(k).wait_recv(), 1)
    total = jnp.zeros((Z * 4, 128), jnp.float32)
    bits = Z.bit_length()
    n_q = NC * 16 // RANK
    for g in (0, 1):
        right = lax.dot_general(fh, dhi[g], NT, preferred_element_type=jnp.float32)
        right = right + lax.dot_general(fh, dlo[g], NT, preferred_element_type=jnp.float32)
        left = left_all[yl if g == 0 else 1 - yl].reshape(NC * 16, T)
        contrib = (left * right).reshape(n_q, RANK, T).sum(axis=1)
        dest, slot = keys[2 * g], keys[2 * g + 1]
        there = (dest >> 1 & Z - 1) * 4 + (dest >> bits) * 2 + (dest & 1)
        wide = jnp.concatenate([contrib] * (128 // n_q), axis=0)
        slot_of = lax.div(lax.broadcasted_iota(jnp.int32, (128, T), 0), n_q)
        wide = jnp.where(slot_of == slot, wide, 0.0)
        place = lax.broadcasted_iota(jnp.int32, (Z * 4, T), 0)
        named = jnp.where(place == there, 1.0, 0.0).astype(jnp.bfloat16)
        high = wide.astype(jnp.bfloat16)
        rest = wide - high.astype(jnp.float32)
        mid = rest.astype(jnp.bfloat16)
        low = (rest - mid.astype(jnp.float32)).astype(jnp.bfloat16)
        for part in (high, mid, low):
            total = total + lax.dot_general(named, part, NT, preferred_element_type=jnp.float32)
    for i in range(Z):
        terms[i] = total[i * 4 : i * 4 + 4]

    def t1(k):
        return remote(terms.at[lax.rem(z + k, Z)], t1_in.at[k], t1_s.at[k], t1_r.at[k], zpeer(k))

    def t2(k):
        return remote(psum, t2_in.at[k], t2_s.at[k], t2_r.at[k], plane(k))

    loop(Z, lambda k: t1(k).start(), 1)

    def add1(k, total):
        t1(k).wait_recv()
        return total + t1_in[k]

    mine = lax.fori_loop(1, Z, add1, terms[z])
    psum[...] = mine
    loop(NPL, lambda k: t2(k).start(), 1)

    def add2(k, total):
        t2(k).wait_recv()
        return total + t2_in[k]

    mine = lax.fori_loop(1, NPL, add2, mine)
    row = lax.broadcasted_iota(jnp.int32, (4, 128), 0)
    scores = jnp.sum(jnp.where(row == quarter, mine, 0.0), axis=0, keepdims=True)
    for e in range(EX_OUT):
        out[e : e + 1, :] = scores[:, e * n_q : (e + 1) * n_q]

    for cp in (pair_w, pair_routes, pair_slots, pair_hg, fh_sib):
        cp.wait_send()
    for direction in (0, 1):
        for a in (0, 1):
            for s in range(1, hops(direction, a) + 1):
                ring(direction, a, s).wait_send()
                sib(direction, a, s).wait_send()
    for a in (0, 1):
        sib(0, a, 0).wait_send()
    for direction in (0, 1):
        for s in range(1 - direction, S + 1 - direction):
            for h in (0, 1):
                tok(direction, s, h).wait_send()
    for k in (1, 2, 3):
        for cp in quad(k):
            cp.wait_send()
        fq(k).wait_send()
    stages_sent()

    loop(NPL // 2, lambda k: lf(k).wait_send(), 1)
    loop(Z, lambda k: t1(k).wait_send(), 1)
    loop(NPL, lambda k: t2(k).wait_send(), 1)


def body(X, YH, Z, tokens, hidden_grad, w_in, b_in, query_in, query_hidden, owners, routes, example_slot):
    T, D = tokens.shape
    M = query_in.shape[0]
    NB = X * YH * 16 // M
    H = w_in.shape[1] // 2
    QC = H // 2
    NC = 2 * NB
    NY, S = 2 * YH, Z // 2
    NPL = X * NY * 2
    NH = Z // 4
    bf, f32 = jnp.bfloat16, jnp.float32
    dma = pltpu.SemaphoreType.DMA
    vmem = pl.BlockSpec(memory_space=pltpu.VMEM)
    anywhere = pl.BlockSpec(memory_space=pl.ANY)
    scratch = [
        pltpu.SMEM(owners.shape, jnp.int32),
        pltpu.VMEM((T, D), bf),
        pltpu.VMEM((T, H), bf),
        pltpu.VMEM((1, H), f32),
        pltpu.VMEM((4, 1, T), jnp.int32),
        pltpu.VMEM((Z, 2, 2, w_in.shape[0], H), bf),
        pltpu.VMEM((T, D), bf),
        pltpu.VMEM((2, T, H), f32),
        pltpu.VMEM((T, H), bf),
        pltpu.VMEM((2, T, H), bf),
        pltpu.VMEM((2, T, H), bf),
        pltpu.VMEM((4, 16, D // 4), bf),
        pltpu.VMEM((4, M, QC), bf),
        pltpu.VMEM((2, NH, 16, 128 + QC), bf),
        pltpu.VMEM((3, NH, 16, 128 + QC), bf),
        pltpu.VMEM((NH, 16, 128 + QC), bf),
        pltpu.VMEM((NH, 16, 128 + QC), bf),
        pltpu.VMEM((2, NH, 16, 128 + QC), bf),
        pltpu.VMEM((2, NH, 16, QC), bf),
        pltpu.VMEM((3, 2, NH, 16, 128), bf),
        pltpu.VMEM((2, X * YH, 16, T), f32),
        pltpu.VMEM((Z, 4, 128), f32),
        pltpu.VMEM((Z, 4, 128), f32),
        pltpu.VMEM((4, 128), f32),
        pltpu.VMEM((NPL, 4, 128), f32),
    ]
    scratch += [dma((2, 2, S + 1))] * 4 + [dma((2, S + 1, 2))] * 2 + [dma((4,))] * 2
    scratch += [dma((2, 4))] * 2 + ([dma((3,))] * 2 + [dma((NH,))] * 4 + [dma((3,))] * 2) + [dma((4,))] * 2
    scratch += [dma((NPL // 2,))] * 2 + [dma((Z,))] * 2 + [dma((NPL,))] * 2 + [dma((9,))]
    return pl.pallas_call(
        functools.partial(kernel, X, YH, Z, NB),
        out_shape=jax.ShapeDtypeStruct((EX_OUT, NC * 16 // RANK), f32),
        in_specs=[anywhere] * 9,
        out_specs=vmem,
        scratch_shapes=scratch,
        compiler_params=pltpu.CompilerParams(
            collective_id=0, has_side_effects=True, vmem_limit_bytes=60 * 2**20
        ),
    )(owners, tokens, hidden_grad, w_in, b_in[None], query_in, query_hidden, routes.reshape(1, T), example_slot[None])


def solution(mesh, YH=2):
    Z = mesh.shape["dp"] // 4
    X = mesh.shape["mp"] // YH
    in_specs = (
        P("dp", None), P("dp", "mp"), P("dp", "mp"), P("mp"), P("dp", None), P("dp", "mp"), P(),
        P("dp", None), P("dp"),
    )
    return jax.shard_map(
        functools.partial(body, X, YH, Z), mesh=mesh, in_specs=in_specs, out_specs=P("dp", None), check_vma=False
    )
```

```python
import functools

import jax
import jax.numpy as jnp
from jax import lax
from jax.experimental import pallas as pl
from jax.experimental.pallas import tpu as pltpu
from jax.sharding import PartitionSpec as P

MESH = pl.DeviceIdType.MESH
RANK = 8
EX_OUT = 8
NT = (((1,), (1,)), ((), ()))


def slope(pre):
    cdf = 0.5 * (1.0 + lax.erf(pre * 0.7071067811865476))
    dens = jnp.exp(-0.5 * pre * pre) * 0.3989422804014327
    return cdf + pre * dens


def kernel(
    X, YH, Z, NB,
    owners_in, tok_in, hg_in, w, bias_in, qi, qh, routes, slots, out,
    owners, tokens, hg, bias, keys,
    wbuf, tok2, acc, hg2, dhi, dlo,
    qi_raw, qh_raw, gbuf, st1, hbuf, st2, fbuf, fsib, fpair, left_all,
    terms, t1_in, psum, t2_in,
    ring_s, ring_r, sib_s, sib_r, tok_s, tok_r, pair_s, pair_r, quad_s, quad_r,
    r1_s, r1_r, r2_s, r2_r, aa_s, aa_r, ab_s, ab_r, fq_s, fq_r, lf_s, lf_r, t1_s, t1_r, t2_s, t2_r, loc_s,
):
    NY, S, NC = 2 * YH, Z // 2, 2 * NB
    T, D = tok_in.shape
    WR, H = w.shape[0], w.shape[1] // 2
    QC = H // 2
    NPL = X * NY * 2
    dp, mp = lax.axis_index("dp"), lax.axis_index("mp")
    c = lax.rem(dp, 2)
    z = lax.rem(lax.div(dp, 2), Z)
    yl = lax.div(dp, 2 * Z)
    yh = lax.rem(mp, YH)
    x = lax.div(mp, YH)
    y = yh * 2 + yl
    me_pl = (x * NY + y) * 2 + c
    quarter = yl * 2 + c

    def dev(x_, y_, z_, c_):
        return ((lax.rem(y_, 2) * Z + z_) * 2 + c_, x_ * YH + lax.div(y_, 2))

    def zpeer(k):
        return dev(x, y, lax.rem(z + k, Z), c)

    def plane(k):
        i = lax.rem(me_pl + k, NPL)
        return dev(lax.div(i, NY * 2), lax.rem(lax.div(i, 2), NY), z, lax.rem(i, 2))

    def remote(src, dst, send, recv, to):
        return pltpu.make_async_remote_copy(
            src_ref=src, dst_ref=dst, send_sem=send, recv_sem=recv,
            device_id=to, device_id_type=MESH,
        )

    def loop(n, f, start=0):
        def step(i, carry):
            f(i)
            return carry

        lax.fori_loop(start, n, step, 0)

    b_mine, h_mine = lax.div(mp, 2), lax.rem(mp, 2)
    qrows = pl.ds(pl.multiple_of(h_mine * 16, 16), 16)

    def half(i):
        return pl.ds(pl.multiple_of(i * H, H), H)

    locals_ = [
        (w.at[:, half(yl)], wbuf.at[z, yl, c]),
        (qi.at[qrows, pl.ds(pl.multiple_of(quarter * (D // 4), 128), D // 4)], qi_raw.at[0]),
        (qh.at[:, pl.ds(pl.multiple_of(quarter * QC, 128), QC)], qh_raw.at[0]),
        (owners_in, owners),
        (tok_in, tokens),
        (hg_in.at[:, half(yl)], hg),
        (bias_in.at[:, half(yl)], bias),
        (routes, keys.at[0]),
        (slots, keys.at[1]),
    ]
    own = [pltpu.make_async_copy(src, dst, loc_s.at[i]) for i, (src, dst) in enumerate(locals_)]
    for cp in own:
        cp.start()

    barrier = pltpu.get_barrier_semaphore()
    loop(Z, lambda k: pl.semaphore_signal(barrier, inc=1, device_id=zpeer(k), device_id_type=MESH), 1)
    loop(NPL, lambda k: pl.semaphore_signal(barrier, inc=1, device_id=plane(k), device_id_type=MESH), 1)
    pl.semaphore_wait(barrier, Z - 1 + NPL - 1)

    sibling = dev(x, y, z, 1 - c)
    partner = dev(x, yh * 2 + 1 - yl, z, c)
    up, down = zpeer(1), zpeer(Z - 1)
    y_up = dev(x, lax.rem(y + 1, NY), z, c)
    y_down = dev(x, lax.rem(y + NY - 1, NY), z, c)

    pair_w = remote(w.at[:, half(1 - yl)], wbuf.at[z, yl, c], pair_s.at[0], pair_r.at[0], partner)
    pair_w.start()
    own[0].wait()

    def at(direction, s):
        return lax.rem(z + (Z - s if direction == 0 else s), Z)

    def ring(direction, a, s):
        ref = wbuf.at[at(direction, s - 1), a, c]
        return remote(
            ref, ref, ring_s.at[direction, a, s], ring_r.at[direction, a, s], (up, down)[direction]
        )

    def sib(direction, a, s):
        ref = wbuf.at[at(direction, s), a, c]
        return remote(ref, ref, sib_s.at[direction, a, s], sib_r.at[direction, a, s], sibling)

    def hops(direction, a):
        return S if direction == a else S - 1

    def cols(direction, s, h):
        return pl.ds(pl.multiple_of(h * (D // 2) + at(direction, s) * 2 * WR, 2 * WR), 2 * WR)

    def tok(direction, s, h):
        k = cols(direction, s, h)
        return remote(
            tokens.at[:, k], tok2.at[:, k], tok_s.at[direction, s, h], tok_r.at[direction, s, h],
            (y_up, y_down)[direction],
        )

    def tok_start(direction, s):
        if (1 if direction == 0 else 0) <= s <= (S if direction == 0 else S - 1):
            tok(direction, s, 0).start()
            tok(direction, s, 1).start()

    def first(a):
        ring(0, a, 1).start()
        ring(1, a, 1).start()
        sib(0, a, 0).start()

    first(yl)

    def quad_of(k):
        q = lax.rem(quarter + k, 4)
        return q, dev(x, yh * 2 + lax.div(q, 2), z, lax.rem(q, 2))

    def quad(k):
        q, to = quad_of(k)
        a = remote(
            qi.at[qrows, pl.ds(pl.multiple_of(q * (D // 4), 128), D // 4)], qi_raw.at[k],
            quad_s.at[0, k], quad_r.at[0, k], to,
        )
        b = remote(
            qh.at[:, pl.ds(pl.multiple_of(q * QC, 128), QC)], qh_raw.at[k],
            quad_s.at[1, k], quad_r.at[1, k], to,
        )
        return a, b

    for k in (1, 2, 3):
        for cp in quad(k):
            cp.start()
    pair_routes = remote(routes, keys.at[2], pair_s.at[1], pair_r.at[1], partner)
    pair_routes.start()
    pair_slots = remote(slots, keys.at[3], pair_s.at[3], pair_r.at[3], partner)
    pair_slots.start()

    pair_w.wait_recv()
    first(1 - yl)
    own[4].wait()
    for s in (0, 1, 2):
        tok_start(0, s)
        tok_start(1, s)
    pair_hg = remote(hg_in.at[:, half(1 - yl)], hg2, pair_s.at[2], pair_r.at[2], partner)


    def pick_factors():
        for k in (1, 2, 3):
            for cp in quad(k):
                cp.wait_recv()
        for i in (1, 2, 3):
            own[i].wait()
        srcs = []
        for k in range(4):
            q = lax.rem(quarter + 4 - k, 4)
            srcs.append((lax.div(q, 2) * Z + z) * 2 + lax.rem(q, 2))

        def pick(b, k):
            return jnp.where(owners[b] == srcs[k], 1.0, 0.0).astype(jnp.float32)

        for i in range(NC):
            b, h = i // 2, i % 2
            gi = sum(pick(b_mine, k) * qi_raw[k, :, i * 128 : (i + 1) * 128].astype(jnp.float32) for k in range(4))
            gh = sum(pick(b, k) * qh_raw[k, h * 16 : (h + 1) * 16].astype(jnp.float32) for k in range(4))
            gbuf[i % 2, i // 2, :, :128] = gi.astype(jnp.bfloat16)
            gbuf[i % 2, i // 2, :, 128:] = gh.astype(jnp.bfloat16)

    NH = Z // 4
    even = lax.rem(z, 2) == 0
    group, u0 = lax.rem(lax.div(z, 2), 2), lax.div(z, 4)

    def to_head(n):
        src = gbuf.at[group if n == 0 else 1 - group]
        return remote(src, st1.at[n], r1_s.at[n], r1_r.at[n], zpeer((Z - 1, Z - 2, 1)[n]))

    def between_heads(m):
        return remote(hbuf.at[lax.rem(u0 + m, NH)], st2.at[m], r2_s.at[m], r2_r.at[m], zpeer(4 * m))

    def share(m):
        ref = fbuf.at[group, u0]
        return remote(ref, ref, aa_s.at[m], aa_r.at[m], zpeer(4 * m))

    def share_arrived(m):
        ref = fbuf.at[group, lax.rem(u0 + NH - m, NH)]
        return remote(ref, ref, aa_s.at[m], aa_r.at[m], up)

    def from_head(n):
        ref = fbuf.at[group]
        return remote(ref, ref, ab_s.at[n], ab_r.at[n], zpeer((Z - 1, Z - 2, 1)[n]))

    def head_arrived(n):
        ref = fbuf.at[group if n == 2 else 1 - group]
        return remote(ref, ref, ab_s.at[n], ab_r.at[n], up)

    def when_even(f):
        pl.when(even)(f)

    def when_odd(f):
        pl.when(jnp.logical_not(even))(f)

    def stage1():
        @when_odd
        def _():
            to_head(0).start()
            to_head(2).start()

        @when_even
        def _():
            to_head(1).start()

    def stage2():
        @when_even
        def _():
            total = gbuf[group].astype(jnp.float32)
            for n in range(3):
                to_head(n).wait_recv()
                total = total + st1[n].astype(jnp.float32)
            hbuf[...] = total.astype(jnp.bfloat16)
            for m in range(1, NH):
                between_heads(m).start()

    def stage3():
        @when_even
        def _():
            total = hbuf[u0].astype(jnp.float32)
            for m in range(1, NH):
                between_heads(m).wait_recv()
                total = total + st2[m].astype(jnp.float32)
            fbuf[group, u0] = total.astype(jnp.bfloat16)
            for m in range(1, NH):
                share(m).start()

    def stage4():
        @when_even
        def _():
            for m in range(1, NH):
                share_arrived(m).wait_recv()
            for n in range(3):
                from_head(n).start()

    def stages_sent():
        @when_odd
        def _():
            to_head(0).wait_send()
            to_head(2).wait_send()

        @when_even
        def _():
            to_head(1).wait_send()
            for m in range(1, NH):
                between_heads(m).wait_send()
                share(m).wait_send()
            for n in range(3):
                from_head(n).wait_send()

    def fq(k):
        _, to = quad_of(k)
        return remote(fbuf.at[:, :, :, pl.ds(0, 128)], fpair.at[k - 1], fq_s.at[k], fq_r.at[k], to)

    fh_sib = remote(fbuf.at[:, :, :, pl.ds(128, QC)], fsib, fq_s.at[0], fq_r.at[0], sibling)

    def gather_factors():
        @when_odd
        def _():
            head_arrived(0).wait_recv()
            head_arrived(2).wait_recv()

        @when_even
        def _():
            head_arrived(1).wait_recv()

        fh_sib.start()
        for k in (1, 2, 3):
            fq(k).start()

    def lf(k):
        n_y = NPL // 2
        i = lax.rem(lax.div(me_pl, 2) + k, n_y)
        to = dev(lax.div(i, NY), lax.rem(i, NY), z, c)
        ref = left_all.at[yl, mp]
        return remote(ref, ref, lf_s.at[k], lf_r.at[k], to)

    def lf_arrived(k):
        n_y = NPL // 2
        i = lax.rem(lax.div(me_pl, 2) + n_y - k, n_y)
        ref = left_all.at[lax.rem(i, 2), lax.div(i, NY) * YH + lax.div(lax.rem(i, NY), 2)]
        return remote(ref, ref, lf_s.at[k], lf_r.at[k], up)

    def left_part():
        total = jnp.zeros((16, T), jnp.float32)
        for k in range(4):
            q = lax.rem(quarter + 4 - k, 4)
            if k:
                fq(k).wait_recv()
            f = jnp.concatenate([fbuf[i % 2, i // 2, :, :128] if k == 0 else fpair[k - 1, i % 2, i // 2] for i in range(NC)], axis=1)
            kk = pl.ds(pl.multiple_of(q * (D // 4), D // 4), D // 4)
            total = total + lax.dot_general(f, tokens[:, kk], NT, preferred_element_type=jnp.float32)
        left_all[yl, mp] = total
        loop(NPL // 2, lambda k: lf(k).start(), 1)

    def multiply(direction, s):
        for a in (0, 1):
            if s == 0:
                sib(0, a, 0).wait_recv()
            elif s <= hops(direction, a):
                sib(direction, a, s).wait_recv()
            elif s == S:
                sib(1 - direction, a, s).wait_recv()
        block = wbuf[at(direction, s)].reshape(4 * WR, H)
        k0, k1 = cols(direction, s, 0), cols(direction, s, 1)
        own = jnp.concatenate([tokens[:, k0], tokens[:, k1]], axis=1)
        acc[0] = acc[0] + jnp.dot(own, block, preferred_element_type=jnp.float32)
        tok(direction, s, 0).wait_recv()
        tok(direction, s, 1).wait_recv()
        other = jnp.concatenate([tok2[:, k0], tok2[:, k1]], axis=1)
        acc[1] = acc[1] + jnp.dot(other, block, preferred_element_type=jnp.float32)

    def advance(direction, a, s):
        if s <= hops(direction, a):
            ring(direction, a, s).wait_recv()
            if s + 1 <= hops(direction, a):
                ring(direction, a, s + 1).start()
            sib(direction, a, s).start()

    pick_factors()
    stage1()
    acc[...] = jnp.zeros_like(acc)
    for s in range(1, S + 1):
        if s == S:
            for t in (S - 2, S - 1):
                if t > 0:
                    multiply(0, t)
                if t >= 0:
                    multiply(1, t)
        for direction, a in ((0, 0), (1, 1), (0, 1), (1, 0)):
            advance(direction, a, s)
        if s + 2 <= S:
            tok_start(0, s + 2)
            tok_start(1, s + 2)
        if s == 1:
            stage2()
        if s == min(2, S):
            pair_hg.start()
        if s == min(3, S):
            stage3()
        if s == min(4, S):
            stage4()
        if s == min(5, S):
            gather_factors()
        if s == min(6, S):
            left_part()
        if 2 <= s < S:
            if s > 2:
                multiply(0, s - 2)
            multiply(1, s - 2)
    multiply(0, S)

    pair_hg.wait_recv()
    pair_routes.wait_recv()
    pair_slots.wait_recv()
    for i in (5, 6, 7, 8):
        own[i].wait()
    fh_sib.wait_recv()
    fh_own = jnp.concatenate([fbuf[i % 2, i // 2, :, 128:] for i in range(NC)], axis=0)
    fh_other = jnp.concatenate([fsib[i % 2, i // 2] for i in range(NC)], axis=0)
    fh = jnp.concatenate([jnp.where(c == 0, fh_own, fh_other), jnp.where(c == 0, fh_other, fh_own)], axis=1)
    shift = bias[...]
    rows = 32
    for g in (0, 1):

        def some(i, carry, g=g):
            at_rows = pl.ds(pl.multiple_of(i * rows, rows), rows)
            grads = hg[at_rows, :] if g == 0 else hg2[at_rows, :]
            delta = grads.astype(jnp.float32) * slope(acc[g, at_rows, :] + shift)
            high = delta.astype(jnp.bfloat16)
            dhi[g, at_rows, :] = high
            dlo[g, at_rows, :] = (delta - high.astype(jnp.float32)).astype(jnp.bfloat16)
            return carry

        lax.fori_loop(0, T // rows, some, 0)
    loop(NPL // 2, lambda k: lf_arrived(k).wait_recv(), 1)
    total = jnp.zeros((Z * 4, 128), jnp.float32)
    bits = Z.bit_length()
    n_q = NC * 16 // RANK
    for g in (0, 1):
        right = lax.dot_general(fh, dhi[g], NT, preferred_element_type=jnp.float32)
        right = right + lax.dot_general(fh, dlo[g], NT, preferred_element_type=jnp.float32)
        left = left_all[yl if g == 0 else 1 - yl].reshape(NC * 16, T)
        contrib = (left * right).reshape(n_q, RANK, T).sum(axis=1)
        dest, slot = keys[2 * g], keys[2 * g + 1]
        there = (dest >> 1 & Z - 1) * 4 + (dest >> bits) * 2 + (dest & 1)
        wide = jnp.concatenate([contrib] * (128 // n_q), axis=0)
        slot_of = lax.div(lax.broadcasted_iota(jnp.int32, (128, T), 0), n_q)
        wide = jnp.where(slot_of == slot, wide, 0.0)
        place = lax.broadcasted_iota(jnp.int32, (Z * 4, T), 0)
        named = jnp.where(place == there, 1.0, 0.0).astype(jnp.bfloat16)
        high = wide.astype(jnp.bfloat16)
        rest = wide - high.astype(jnp.float32)
        mid = rest.astype(jnp.bfloat16)
        low = (rest - mid.astype(jnp.float32)).astype(jnp.bfloat16)
        for part in (high, mid, low):
            total = total + lax.dot_general(named, part, NT, preferred_element_type=jnp.float32)
    for i in range(Z):
        terms[i] = total[i * 4 : i * 4 + 4]

    def t1(k):
        return remote(terms.at[lax.rem(z + k, Z)], t1_in.at[k], t1_s.at[k], t1_r.at[k], zpeer(k))

    def t2(k):
        return remote(psum, t2_in.at[k], t2_s.at[k], t2_r.at[k], plane(k))

    t1(S).start()

    def farthest_first(i):
        t1(S + i).start()
        t1(S - i).start()

    loop(S, farthest_first, 1)

    def add1(k, total):
        t1(k).wait_recv()
        return total + t1_in[k]

    mine = lax.fori_loop(1, Z, add1, terms[z])
    psum[...] = mine
    loop(NPL, lambda k: t2(k).start(), 1)

    def add2(k, total):
        t2(k).wait_recv()
        return total + t2_in[k]

    mine = lax.fori_loop(1, NPL, add2, mine)
    row = lax.broadcasted_iota(jnp.int32, (4, 128), 0)
    scores = jnp.sum(jnp.where(row == quarter, mine, 0.0), axis=0, keepdims=True)
    for e in range(EX_OUT):
        out[e : e + 1, :] = scores[:, e * n_q : (e + 1) * n_q]

    for cp in (pair_w, pair_routes, pair_slots, pair_hg, fh_sib):
        cp.wait_send()
    for direction in (0, 1):
        for a in (0, 1):
            for s in range(1, hops(direction, a) + 1):
                ring(direction, a, s).wait_send()
                sib(direction, a, s).wait_send()
    for a in (0, 1):
        sib(0, a, 0).wait_send()
    for direction in (0, 1):
        for s in range(1 - direction, S + 1 - direction):
            for h in (0, 1):
                tok(direction, s, h).wait_send()
    for k in (1, 2, 3):
        for cp in quad(k):
            cp.wait_send()
        fq(k).wait_send()
    stages_sent()

    loop(NPL // 2, lambda k: lf(k).wait_send(), 1)
    loop(Z, lambda k: t1(k).wait_send(), 1)
    loop(NPL, lambda k: t2(k).wait_send(), 1)


def body(X, YH, Z, tokens, hidden_grad, w_in, b_in, query_in, query_hidden, owners, routes, example_slot):
    T, D = tokens.shape
    M = query_in.shape[0]
    NB = X * YH * 16 // M
    H = w_in.shape[1] // 2
    QC = H // 2
    NC = 2 * NB
    NY, S = 2 * YH, Z // 2
    NPL = X * NY * 2
    NH = Z // 4
    bf, f32 = jnp.bfloat16, jnp.float32
    dma = pltpu.SemaphoreType.DMA
    vmem = pl.BlockSpec(memory_space=pltpu.VMEM)
    anywhere = pl.BlockSpec(memory_space=pl.ANY)
    scratch = [
        pltpu.SMEM(owners.shape, jnp.int32),
        pltpu.VMEM((T, D), bf),
        pltpu.VMEM((T, H), bf),
        pltpu.VMEM((1, H), f32),
        pltpu.VMEM((4, 1, T), jnp.int32),
        pltpu.VMEM((Z, 2, 2, w_in.shape[0], H), bf),
        pltpu.VMEM((T, D), bf),
        pltpu.VMEM((2, T, H), f32),
        pltpu.VMEM((T, H), bf),
        pltpu.VMEM((2, T, H), bf),
        pltpu.VMEM((2, T, H), bf),
        pltpu.VMEM((4, 16, D // 4), bf),
        pltpu.VMEM((4, M, QC), bf),
        pltpu.VMEM((2, NH, 16, 128 + QC), bf),
        pltpu.VMEM((3, NH, 16, 128 + QC), bf),
        pltpu.VMEM((NH, 16, 128 + QC), bf),
        pltpu.VMEM((NH, 16, 128 + QC), bf),
        pltpu.VMEM((2, NH, 16, 128 + QC), bf),
        pltpu.VMEM((2, NH, 16, QC), bf),
        pltpu.VMEM((3, 2, NH, 16, 128), bf),
        pltpu.VMEM((2, X * YH, 16, T), f32),
        pltpu.VMEM((Z, 4, 128), f32),
        pltpu.VMEM((Z, 4, 128), f32),
        pltpu.VMEM((4, 128), f32),
        pltpu.VMEM((NPL, 4, 128), f32),
    ]
    scratch += [dma((2, 2, S + 1))] * 4 + [dma((2, S + 1, 2))] * 2 + [dma((4,))] * 2
    scratch += [dma((2, 4))] * 2 + ([dma((3,))] * 2 + [dma((NH,))] * 4 + [dma((3,))] * 2) + [dma((4,))] * 2
    scratch += [dma((NPL // 2,))] * 2 + [dma((Z,))] * 2 + [dma((NPL,))] * 2 + [dma((9,))]
    return pl.pallas_call(
        functools.partial(kernel, X, YH, Z, NB),
        out_shape=jax.ShapeDtypeStruct((EX_OUT, NC * 16 // RANK), f32),
        in_specs=[anywhere] * 9,
        out_specs=vmem,
        scratch_shapes=scratch,
        compiler_params=pltpu.CompilerParams(
            collective_id=0, has_side_effects=True, vmem_limit_bytes=60 * 2**20
        ),
    )(owners, tokens, hidden_grad, w_in, b_in[None], query_in, query_hidden, routes.reshape(1, T), example_slot[None])


def solution(mesh, YH=2):
    Z = mesh.shape["dp"] // 4
    X = mesh.shape["mp"] // YH
    in_specs = (
        P("dp", None), P("dp", "mp"), P("dp", "mp"), P("mp"), P("dp", None), P("dp", "mp"), P(),
        P("dp", None), P("dp"),
    )
    return jax.shard_map(
        functools.partial(body, X, YH, Z), mesh=mesh, in_specs=in_specs, out_specs=P("dp", None), check_vma=False
    )
```
